32 devices in a mesh: vgroup: 2 (over x), feat: 16 (over z, y, core).
Axes of the slice: x: 2, y: 2, z: 4, core: 2. Of those that a mesh axis runs over, the one named last changes fastest.
Arguments:
- features_t: bfloat16 [2, 1024, 16384], P('vgroup', 'feat'), may hold values from -6 to 6
- tile_weights: bfloat16 [2, 512, 128, 128], P('vgroup'), may hold values from -0.1875 to 0.1875
- tile_dst: int32 [2, 512], P('vgroup'), may hold values from 0 to 63
- tile_src: int32 [2, 512], P('vgroup'), may hold values from 0 to 127
- tile_count: int32 [2], P('vgroup'), may hold values from 128 to 512, as said below
- w_self: bfloat16 [1024, 256], P('feat'), may hold values from -0.1875 to 0.1875
- w_neigh: bfloat16 [1024, 256], P('feat'), may hold values from -0.1875 to 0.1875
- bias: float32 [256], replicated, may hold values from -4 to 4
- grad_hidden: bfloat16 [16384, 256], P(('vgroup', 'feat')), may hold values from -1 to 1
Outputs:
- hidden: bfloat16 [16384, 256], P(('vgroup', 'feat'))
- grad_self: float32 [1024, 256], P('feat')
- grad_neigh: float32 [1024, 256], P('feat')
- grad_bias: float32 [256], replicated
The draws below stay inside these ranges and needn't reach their ends.
Inputs may be any that keep to these rules, and one draw needn't show every extreme that they name: `tile_count`: slots at or past a group's count are ignored; at least one group has all 512 slots live.
All inputs are finite; a program needn't handle non-finite values.
Results may differ from the reference program's by a relative error of at most 0.0075.
Values may be sent and summed in bfloat16 or wider, within the bound.
A program may use at most 192 MiB of HBM per device.

```python
import jax
import jax.numpy as jnp
from jax import lax

F = 1024
H = 256
TILE = 128
TPR = 8
GROUPS = 2
NDST = 8192
DT = 64
ST = 128
NSRC = 16384
TILES = 512
ROWS = 16384


def draw_tile_count(key, part):
    base = jax.random.fold_in(key, 11)
    first_key, second_key = jax.random.split(base)
    counts = jax.random.randint(first_key, (GROUPS,), TILES // 4, TILES + 1)
    full_group = jax.random.randint(second_key, (), 0, GROUPS)
    return jnp.where(jnp.arange(GROUPS) == full_group, TILES, counts).astype(jnp.int32)


def set_ends(values, stream_key, smallest, largest):
    longest = values.shape.index(max(values.shape))
    spots = []
    for shift in (0, 1):
        where = [jax.random.randint(jax.random.fold_in(stream_key, axis), (), 0, length) for axis, length in enumerate(values.shape)]
        where[longest] = (where[longest] + shift) % values.shape[longest]
        spots.append(tuple(where))
    return values.at[spots[0]].set(smallest).at[spots[1]].set(largest)


def block_scale(stream_key, dims, shards, smallest, top_value):
    factor_of = 1.0
    for dim, shards_of in shards:
        heights = jax.random.uniform(jax.random.fold_in(jax.random.fold_in(stream_key, 6), dim), (shards_of,), jnp.float32, smallest / len(shards), top_value / len(shards))
        factor_of = factor_of * jnp.repeat(jnp.exp(heights), dims[dim] // shards_of).reshape((-1,) + (1,) * (len(dims) - 1 - dim))
    return factor_of


def noise(own_key, dims, spread, reach, cuts=(), kind=jnp.bfloat16):
    values = jax.random.normal(own_key, dims, jnp.float32) * spread
    if len(cuts) > 0:
        values = block_scale(own_key, dims, cuts, -0.22, 0.18) * values
    return jnp.clip(values, min=-reach, max=reach).astype(kind)


def setup_inputs(seed: int = 0) -> dict:
    key_list = jax.random.split(jax.random.key(seed), 10)
    return {
        "features_t": noise(key_list[0], (GROUPS, F, NSRC), 1.0, 6.0, ((0, 2), (1, 16))),
        "tile_weights": noise(key_list[1], (GROUPS, TILES, TILE, TILE), (TPR * TILE) ** -0.5, 0.1875, ((0, 2),)),
        "tile_dst": set_ends(jax.random.randint(key_list[2], (GROUPS, TILES), 0, DT), jax.random.fold_in(key_list[2], 1), 0, DT - 1).astype(jnp.int32),
        "tile_src": set_ends(jax.random.randint(key_list[3], (GROUPS, TILES), 0, ST), jax.random.fold_in(key_list[3], 1), 0, ST - 1).astype(jnp.int32),
        "tile_count": draw_tile_count(jax.random.fold_in(key_list[9], 71), 0),
        "w_self": noise(key_list[5], (F, H), F ** -0.5, 0.1875, ((0, 16),)),
        "w_neigh": noise(key_list[6], (F, H), F ** -0.5, 0.1875, ((0, 16),)),
        "bias": noise(key_list[7], (H,), 1.0, 4.0, (), jnp.float32),
        "grad_hidden": noise(key_list[8], (ROWS, H), 0.0625, 1.0, ((0, 32),)),
    }


def activate(pre):
    return jax.nn.gelu(pre, approximate=True)

def reference(features_t, tile_weights, tile_dst, tile_src, tile_count, w_self, w_neigh, bias, grad_hidden):
    upstream_all = grad_hidden.reshape(GROUPS, NDST, H)

    def one_group(items):
        feats, weights, dsts, srcs, count, upstream = items
        blocks = feats.reshape(F, ST, TILE)[:, srcs, :]
        product = jnp.einsum('ftk,tjk->ftj', blocks.astype(jnp.float32), weights.astype(jnp.float32))
        live = (jnp.arange(TILES) < count).astype(jnp.float32)
        onehot = (dsts[None, :] == jnp.arange(DT)[:, None]).astype(jnp.float32) * live[None, :]
        summed = jnp.einsum('dt,ftj->fdj', onehot, product, precision=lax.Precision.HIGHEST)
        aggregated = summed.reshape(F, NDST).astype(jnp.bfloat16)
        target_columns = feats[:, :NDST]
        pre = jnp.dot(target_columns.T, w_self, preferred_element_type=jnp.float32)
        pre = pre + jnp.dot(aggregated.T, w_neigh, preferred_element_type=jnp.float32) + bias
        output, pullback = jax.vjp(activate, pre)
        delta = pullback(upstream.astype(jnp.float32))[0].astype(jnp.bfloat16)
        grad_s = jnp.dot(target_columns, delta, preferred_element_type=jnp.float32)
        grad_n = jnp.dot(aggregated, delta, preferred_element_type=jnp.float32)
        grad_b = lax.optimization_barrier(jnp.sum(delta.astype(jnp.float32), axis=0))
        return (output.astype(jnp.bfloat16), grad_s, grad_n, grad_b)
    hidden, grad_s, grad_n, grad_b = lax.map(one_group, (features_t, tile_weights, tile_dst, tile_src, tile_count, upstream_all))
    return (hidden.reshape(GROUPS * NDST, H), lax.optimization_barrier(jnp.sum(grad_s, axis=0)), lax.optimization_barrier(jnp.sum(grad_n, axis=0)), lax.optimization_barrier(jnp.sum(grad_b, axis=0)))
```

```python
import functools

import jax
import jax.numpy as jnp
from jax import lax
from jax.experimental import pallas as pl
from jax.experimental.pallas import tpu as pltpu
from jax.sharding import PartitionSpec as P

STEP = 64
UNROLL = 8


def aggregate_kernel(dst_ref, src_ref, count_ref, x_ref, w_ref, out_ref, acc_ref):
    step = pl.program_id(0)
    tile = w_ref.shape[1]
    dtiles = out_ref.shape[1] // tile

    @pl.when(step == 0)
    def _():
        acc_ref[...] = jnp.zeros_like(acc_ref)

    @pl.loop(0, STEP // UNROLL)
    def _(group):
        for k in range(UNROLL):
            i = group * UNROLL + k
            t = step * STEP + i
            d = jnp.where(t < count_ref[0], dst_ref[t], dtiles)
            s = pl.multiple_of(src_ref[t] * tile, tile)
            prod = lax.dot_general(
                x_ref[:, pl.ds(s, tile)], w_ref[i], (((1,), (1,)), ((), ())),
                preferred_element_type=jnp.float32,
            )
            acc_ref[d] = acc_ref[d] + prod

    @pl.when(step == pl.num_programs(0) - 1)
    def _():
        for d in range(dtiles):
            out_ref[:, d * tile:(d + 1) * tile] = acc_ref[d].astype(out_ref.dtype)


def aggregate(feats, tiles, dsts, srcs, count, ndst):
    fcols, nsrc = feats.shape
    total, tile, _ = tiles.shape
    return pl.pallas_call(
        aggregate_kernel,
        grid_spec=pltpu.PrefetchScalarGridSpec(
            num_scalar_prefetch=3,
            grid=(total // STEP,),
            in_specs=[
                pl.BlockSpec((fcols, nsrc), lambda i, *_: (0, 0), pipeline_mode=pl.Buffered(1)),
                pl.BlockSpec((STEP, tile, tile), lambda i, *_: (i, 0, 0)),
            ],
            out_specs=pl.BlockSpec((fcols, ndst), lambda i, *_: (0, 0), pipeline_mode=pl.Buffered(1)),
            scratch_shapes=[pltpu.VMEM((ndst // tile + 1, fcols, tile), jnp.float32)],
        ),
        out_shape=jax.ShapeDtypeStruct((fcols, ndst), jnp.bfloat16),
        compiler_params=pltpu.CompilerParams(vmem_limit_bytes=40 * 2**20),
        cost_estimate=pl.CostEstimate(
            flops=2 * total * fcols * tile * tile, bytes_accessed=total * tile * tile * 2,
            transcendentals=0,
        ),
        name="aggregate",
    )(dsts, srcs, count, feats, tiles)


MERGE = 8
CUBIC = 0.044715
ROOT = 0.7978845608


def exchange_kernel(
    groups, nfeat,
    x_ref, a_ref, ws_ref, wn_ref, bias_ref, up_ref,
    hidden_ref, gs_ref, gn_ref, gb_ref,
    xm, am, wm, psend, precv, dall, gacc, gsend, grecv, vsend, vrecv,
    x_sems, a_sems, w_sems, p_sems, d_sems, g_sems, v_sems, l_sems,
):
    outer = nfeat // MERGE
    fcols = ws_ref.shape[0]
    rows = up_ref.shape[0]
    width = up_ref.shape[1]
    grp = lax.axis_index("vgroup")
    me = lax.axis_index("feat")
    lo = lax.rem(me, MERGE)
    hi = lax.div(me, MERGE)

    def inner_peer(k):
        return (grp, hi * MERGE + (lo ^ k))

    def outer_peer(j):
        return (grp, (hi ^ j) * MERGE + lo)

    def group_peer(j):
        return (grp ^ j, me)

    peers = [inner_peer(k) for k in range(1, MERGE)]
    peers += [outer_peer(j) for j in range(1, outer)]
    peers += [group_peer(j) for j in range(1, groups)]
    barrier = pltpu.get_barrier_semaphore()
    for peer in peers:
        pl.semaphore_signal(barrier, inc=1, device_id=peer, device_id_type=pl.DeviceIdType.MESH)
    pl.semaphore_wait(barrier, len(peers))

    def remote(source, target, sems, index, peer):
        copy = pltpu.make_async_remote_copy(
            src_ref=source, dst_ref=target,
            send_sem=sems.at[(0,) + index], recv_sem=sems.at[(1,) + index],
            device_id=peer, device_id_type=pl.DeviceIdType.MESH,
        )
        copy.start()
        return copy

    def columns(j, k):
        owner = (hi ^ j) * MERGE + (lo ^ k)
        return pl.ds(pl.multiple_of(owner * rows, rows), rows)

    order = list(range(1, outer)) + [0]
    pending = []
    local = []
    got_w = []
    for i, weights in enumerate((ws_ref, wn_ref)):
        own = pltpu.make_async_copy(weights, wm.at[i, 0], l_sems.at[0, i])
        own.start()
        local.append(own)
        for k in range(1, MERGE):
            got_w.append(remote(weights, wm.at[i, k], w_sems, (i, k), inner_peer(k)))
    got = {}
    for j in order:
        got[j] = []
        for i, (whole, merged, sems) in enumerate(((x_ref, xm, x_sems), (a_ref, am, a_sems))):
            own = pltpu.make_async_copy(
                whole.at[:, columns(j, 0)], merged.at[j, 0], l_sems.at[1 + j, i])
            own.start()
            local.append(own)
            for k in range(1, MERGE):
                got[j].append(remote(
                    whole.at[:, columns(j, k)], merged.at[j, k], sems, (j, k), inner_peer(k)))
    for copy in local:
        copy.wait()
    for copy in got_w:
        copy.wait_recv()
    pending += got_w

    merged_cols = MERGE * fcols

    def partial_pre(j):
        for copy in got[j]:
            copy.wait_recv()
        pending.extend(got[j])
        total = lax.dot_general(
            xm[j].reshape(merged_cols, rows), wm[0].reshape(merged_cols, width),
            (((0,), (0,)), ((), ())), preferred_element_type=jnp.float32)
        return total + lax.dot_general(
            am[j].reshape(merged_cols, rows), wm[1].reshape(merged_cols, width),
            (((0,), (0,)), ((), ())), preferred_element_type=jnp.float32)

    sent = []
    for j in range(1, outer):
        psend[j] = partial_pre(j).astype(psend.dtype)
        sent.append(remote(psend.at[j], precv.at[j], p_sems, (j,), outer_peer(j)))
    pre = partial_pre(0) + bias_ref[...]
    for j in range(1, outer):
        sent[j - 1].wait_recv()
        pre = pre + precv[j].astype(jnp.float32)
    pending += sent
    square = pre * pre
    t = jnp.tanh(ROOT * pre * (1.0 + CUBIC * square))
    half = 0.5 * (1.0 + t)
    hidden_ref[...] = (pre * half).astype(hidden_ref.dtype)
    slope = half + 0.5 * pre * (1.0 - t * t) * (ROOT * (1.0 + 3.0 * CUBIC * square))
    dall[0] = (slope * up_ref[...].astype(jnp.float32)).astype(dall.dtype)
    sent = [remote(dall.at[0], dall.at[j], d_sems, (j,), outer_peer(j)) for j in range(1, outer)]

    colsum = jnp.zeros((1, width), jnp.float32)
    for j in range(outer):
        if j > 0:
            sent[j - 1].wait_recv()
        delta = dall[j]
        colsum = colsum + jnp.sum(delta.astype(jnp.float32), axis=0, keepdims=True)
        for i, merged in enumerate((xm, am)):
            part = jnp.dot(
                merged[j].reshape(merged_cols, rows), delta, preferred_element_type=jnp.float32
            ).reshape(MERGE, fcols, width)
            if j == 0:
                gacc[i] = part
            else:
                gacc[i] = gacc[i] + part
    pending += sent
    high = colsum.astype(jnp.bfloat16)
    low = (colsum - high.astype(jnp.float32)).astype(jnp.bfloat16)
    row_id = lax.broadcasted_iota(jnp.int32, (16, width), 0)
    tag = jnp.where(
        row_id == 0, high.astype(jnp.float32),
        jnp.where(row_id == 1, low.astype(jnp.float32), 0.0)).astype(jnp.bfloat16)
    sent = []
    for k in range(1, MERGE):
        gsend[k, 0:fcols] = gacc[0, k].astype(gsend.dtype)
        gsend[k, fcols:2 * fcols] = gacc[1, k].astype(gsend.dtype)
        gsend[k, 2 * fcols:2 * fcols + 16] = tag
        sent.append(remote(gsend.at[k], grecv.at[k], g_sems, (k,), inner_peer(k)))
    total_s = gacc[0, 0]
    total_n = gacc[1, 0]
    total_b = jnp.where(row_id == 0, colsum, 0.0)
    for k in range(1, MERGE):
        sent[k - 1].wait_recv()
        total_s = total_s + grecv[k, 0:fcols].astype(jnp.float32)
        total_n = total_n + grecv[k, fcols:2 * fcols].astype(jnp.float32)
        total_b = total_b + grecv[k, 2 * fcols:2 * fcols + 16].astype(jnp.float32)
    pending += sent
    vsend[0:fcols] = total_s
    vsend[fcols:2 * fcols] = total_n
    vsend[2 * fcols:2 * fcols + 16] = total_b
    sent = [remote(vsend, vrecv.at[j], v_sems, (j,), group_peer(j)) for j in range(1, groups)]
    for j in range(1, groups):
        sent[j - 1].wait_recv()
        total_s = total_s + vrecv[j, 0:fcols]
        total_n = total_n + vrecv[j, fcols:2 * fcols]
        total_b = total_b + vrecv[j, 2 * fcols:2 * fcols + 16]
    pending += sent
    gs_ref[...] = total_s
    gn_ref[...] = total_n
    gb_ref[...] = jnp.sum(total_b, axis=0, keepdims=True)
    for copy in pending:
        copy.wait_send()


def exchange(feats, aggregated, w_self, w_neigh, bias, upstream):
    groups = lax.axis_size("vgroup")
    nfeat = lax.axis_size("feat")
    outer = nfeat // MERGE
    fcols, width = w_self.shape
    rows = upstream.shape[0]
    any_spec = pl.BlockSpec(memory_space=pl.ANY)
    vmem_spec = pl.BlockSpec(memory_space=pltpu.VMEM)
    dma = pltpu.SemaphoreType.DMA
    return pl.pallas_call(
        functools.partial(exchange_kernel, groups, nfeat),
        out_shape=(
            jax.ShapeDtypeStruct((rows, width), jnp.bfloat16),
            jax.ShapeDtypeStruct((fcols, width), jnp.float32),
            jax.ShapeDtypeStruct((fcols, width), jnp.float32),
            jax.ShapeDtypeStruct((1, width), jnp.float32),
        ),
        in_specs=[any_spec] * 4 + [vmem_spec] * 2,
        out_specs=(vmem_spec,) * 4,
        scratch_shapes=[
            pltpu.VMEM((outer, MERGE, fcols, rows), jnp.bfloat16),
            pltpu.VMEM((outer, MERGE, fcols, rows), jnp.bfloat16),
            pltpu.VMEM((2, MERGE, fcols, width), jnp.bfloat16),
            pltpu.VMEM((outer, rows, width), jnp.bfloat16),
            pltpu.VMEM((outer, rows, width), jnp.bfloat16),
            pltpu.VMEM((outer, rows, width), jnp.bfloat16),
            pltpu.VMEM((2, MERGE, fcols, width), jnp.float32),
            pltpu.VMEM((MERGE, 2 * fcols + 16, width), jnp.bfloat16),
            pltpu.VMEM((MERGE, 2 * fcols + 16, width), jnp.bfloat16),
            pltpu.VMEM((2 * fcols + 16, width), jnp.float32),
            pltpu.VMEM((groups, 2 * fcols + 16, width), jnp.float32),
            dma((2, outer, MERGE)),
            dma((2, outer, MERGE)),
            dma((2, 2, MERGE)),
            dma((2, outer)),
            dma((2, outer)),
            dma((2, MERGE)),
            dma((2, groups)),
            dma((1 + outer, 2)),
        ],
        compiler_params=pltpu.CompilerParams(
            collective_id=0, has_side_effects=True, vmem_limit_bytes=40 * 2**20),
        name="exchange",
    )(feats, aggregated, w_self, w_neigh, bias.reshape(1, width), upstream)


def body(
    features_t, tile_weights, tile_dst, tile_src, tile_count, w_self, w_neigh, bias, grad_hidden
):
    feats = features_t[0]
    ndst = grad_hidden.shape[0] * lax.axis_size("feat")
    aggregated = aggregate(feats, tile_weights[0], tile_dst[0], tile_src[0], tile_count, ndst)
    hidden, grad_self, grad_neigh, grad_bias = exchange(
        feats, aggregated, w_self, w_neigh, bias, grad_hidden)
    return (hidden, grad_self, grad_neigh, grad_bias[0])


def solution(mesh):
    return jax.shard_map(
        body,
        mesh=mesh,
        in_specs=(
            P("vgroup", "feat", None),
            P("vgroup", None, None, None),
            P("vgroup", None),
            P("vgroup", None),
            P("vgroup"),
            P("feat", None),
            P("feat", None),
            P(),
            P(("vgroup", "feat"), None),
        ),
        out_specs=(P(("vgroup", "feat"), None), P("feat", None), P("feat", None), P()),
        check_vma=False,
    )
```

```python
import functools

import jax
import jax.numpy as jnp
from jax import lax
from jax.experimental import pallas as pl
from jax.experimental.pallas import tpu as pltpu
from jax.sharding import PartitionSpec as P

STEP = 64
HALF = 16


def aggregate_kernel(dst_ref, src_ref, count_ref, x_ref, w_ref, out_ref, acc_a, acc_b, buf_a, buf_b):
    step = pl.program_id(0)
    tile = w_ref.shape[1]
    dtiles = out_ref.shape[1] // tile
    base = step * STEP

    @pl.when(step == 0)
    def _():
        acc_a[...] = jnp.zeros_like(acc_a)
        acc_b[...] = jnp.zeros_like(acc_b)
        buf_b[...] = jnp.zeros_like(buf_b)

    def multiply(first, buf):
        for k in range(HALF):
            s = pl.multiple_of(src_ref[base + first + k] * tile, tile)
            buf[k] = lax.dot_general(
                x_ref[:, pl.ds(s, tile)], w_ref[first + k], (((1,), (1,)), ((), ())),
                preferred_element_type=jnp.float32,
            )

    def add(first, buf):
        for k in range(HALF):
            t = first + k
            live = jnp.logical_and(t >= 0, t < count_ref[0])
            d = jnp.where(live, dst_ref[jnp.maximum(t, 0)], dtiles)
            acc = (acc_a, acc_b)[k % 2]
            acc[d] = acc[d] + buf[k]

    @pl.loop(0, STEP // (2 * HALF))
    def _(pair):
        first = pair * 2 * HALF
        multiply(first, buf_a)
        add(base + first - HALF, buf_b)
        multiply(first + HALF, buf_b)
        add(base + first, buf_a)

    @pl.when(step == pl.num_programs(0) - 1)
    def _():
        add(base + STEP - HALF, buf_b)
        for d in range(dtiles):
            out_ref[:, d * tile:(d + 1) * tile] = (acc_a[d] + acc_b[d]).astype(out_ref.dtype)


def aggregate(feats, tiles, dsts, srcs, count, ndst):
    fcols, nsrc = feats.shape
    total, tile, _ = tiles.shape
    return pl.pallas_call(
        aggregate_kernel,
        grid_spec=pltpu.PrefetchScalarGridSpec(
            num_scalar_prefetch=3,
            grid=(total // STEP,),
            in_specs=[
                pl.BlockSpec((fcols, nsrc), lambda i, *_: (0, 0), pipeline_mode=pl.Buffered(1)),
                pl.BlockSpec((STEP, tile, tile), lambda i, *_: (i, 0, 0)),
            ],
            out_specs=pl.BlockSpec((fcols, ndst), lambda i, *_: (0, 0), pipeline_mode=pl.Buffered(1)),
            scratch_shapes=[pltpu.VMEM((ndst // tile + 1, fcols, tile), jnp.float32)] * 2
            + [pltpu.VMEM((HALF, fcols, tile), jnp.float32)] * 2,
        ),
        out_shape=jax.ShapeDtypeStruct((fcols, ndst), jnp.bfloat16),
        compiler_params=pltpu.CompilerParams(vmem_limit_bytes=40 * 2**20),
        cost_estimate=pl.CostEstimate(
            flops=2 * total * fcols * tile * tile, bytes_accessed=total * tile * tile * 2,
            transcendentals=0,
        ),
        name="aggregate",
    )(dsts, srcs, count, feats, tiles)


MERGE = 8
CUBIC = 0.044715
ROOT = 0.7978845608


def exchange_kernel(
    groups, nfeat,
    x_ref, a_ref, ws_ref, wn_ref, bias_ref, up_ref,
    hidden_ref, gs_ref, gn_ref, gb_ref,
    xm, am, wm, psend, precv, dall, gacc, gsend, grecv, vsend, vrecv,
    x_sems, a_sems, w_sems, p_sems, d_sems, g_sems, v_sems, l_sems,
):
    outer = nfeat // MERGE
    fcols = ws_ref.shape[0]
    rows = up_ref.shape[0]
    width = up_ref.shape[1]
    grp = lax.axis_index("vgroup")
    me = lax.axis_index("feat")
    lo = lax.rem(me, MERGE)
    hi = lax.div(me, MERGE)

    def inner_peer(k):
        return (grp, hi * MERGE + (lo ^ k))

    def outer_peer(j):
        return (grp, (hi ^ j) * MERGE + lo)

    def group_peer(j):
        return (grp ^ j, me)

    peers = [inner_peer(k) for k in range(1, MERGE)]
    peers += [outer_peer(j) for j in range(1, outer)]
    peers += [group_peer(j) for j in range(1, groups)]
    barrier = pltpu.get_barrier_semaphore()
    for peer in peers:
        pl.semaphore_signal(barrier, inc=1, device_id=peer, device_id_type=pl.DeviceIdType.MESH)
    pl.semaphore_wait(barrier, len(peers))

    def remote(source, target, sems, index, peer):
        copy = pltpu.make_async_remote_copy(
            src_ref=source, dst_ref=target,
            send_sem=sems.at[(0,) + index], recv_sem=sems.at[(1,) + index],
            device_id=peer, device_id_type=pl.DeviceIdType.MESH,
        )
        copy.start()
        return copy

    def columns(j, k):
        owner = (hi ^ j) * MERGE + (lo ^ k)
        return pl.ds(pl.multiple_of(owner * rows, rows), rows)

    order = list(range(1, outer)) + [0]
    pending = []
    local = []
    got_w = []
    for i, weights in enumerate((ws_ref, wn_ref)):
        own = pltpu.make_async_copy(weights, wm.at[i, 0], l_sems.at[0, i])
        own.start()
        local.append(own)
        for k in range(1, MERGE):
            if k == 1 or k % 2 == 0:
                got_w.append(remote(weights, wm.at[i, k], w_sems, (i, k), inner_peer(k)))
    got = {}
    for j in order:
        got[j] = []
        for i, (whole, merged, sems) in enumerate(((x_ref, xm, x_sems), (a_ref, am, a_sems))):
            own = pltpu.make_async_copy(
                whole.at[:, columns(j, 0)], merged.at[j, 0], l_sems.at[1 + j, i])
            own.start()
            local.append(own)
            for k in range(1, MERGE):
                got[j].append(remote(
                    whole.at[:, columns(j, k)], merged.at[j, k], sems, (j, k), inner_peer(k)))
    for copy in local:
        copy.wait()
    for copy in got_w:
        copy.wait_recv()
    pending += got_w
    got_w = [
        remote(wm.at[i, k - 1], wm.at[i, k], w_sems, (i, k), inner_peer(1))
        for i in range(2) for k in range(3, MERGE, 2)
    ]
    for copy in got_w:
        copy.wait_recv()
    pending += got_w

    merged_cols = MERGE * fcols

    def partial_pre(j):
        for copy in got[j]:
            copy.wait_recv()
        pending.extend(got[j])
        total = lax.dot_general(
            xm[j].reshape(merged_cols, rows), wm[0].reshape(merged_cols, width),
            (((0,), (0,)), ((), ())), preferred_element_type=jnp.float32)
        return total + lax.dot_general(
            am[j].reshape(merged_cols, rows), wm[1].reshape(merged_cols, width),
            (((0,), (0,)), ((), ())), preferred_element_type=jnp.float32)

    sent = []
    for j in range(1, outer):
        psend[j] = partial_pre(j).astype(psend.dtype)
        sent.append(remote(psend.at[j], precv.at[j], p_sems, (j,), outer_peer(j)))
    pre = partial_pre(0) + bias_ref[...]
    for j in range(1, outer):
        sent[j - 1].wait_recv()
        pre = pre + precv[j].astype(jnp.float32)
    pending += sent
    square = pre * pre
    t = jnp.tanh(ROOT * pre * (1.0 + CUBIC * square))
    half = 0.5 * (1.0 + t)
    hidden_ref[...] = (pre * half).astype(hidden_ref.dtype)
    slope = half + 0.5 * pre * (1.0 - t * t) * (ROOT * (1.0 + 3.0 * CUBIC * square))
    dall[0] = (slope * up_ref[...].astype(jnp.float32)).astype(dall.dtype)
    sent = [remote(dall.at[0], dall.at[j], d_sems, (j,), outer_peer(j)) for j in range(1, outer)]

    colsum = jnp.zeros((1, width), jnp.float32)
    for j in range(outer):
        if j > 0:
            sent[j - 1].wait_recv()
        delta = dall[j]
        colsum = colsum + jnp.sum(delta.astype(jnp.float32), axis=0, keepdims=True)
        for i, merged in enumerate((xm, am)):
            part = jnp.dot(
                merged[j].reshape(merged_cols, rows), delta, preferred_element_type=jnp.float32
            ).reshape(MERGE, fcols, width)
            if j == 0:
                gacc[i] = part
            else:
                gacc[i] = gacc[i] + part
    pending += sent
    high = colsum.astype(jnp.bfloat16)
    low = (colsum - high.astype(jnp.float32)).astype(jnp.bfloat16)
    row_id = lax.broadcasted_iota(jnp.int32, (16, width), 0)
    tag = jnp.where(
        row_id == 0, high.astype(jnp.float32),
        jnp.where(row_id == 1, low.astype(jnp.float32), 0.0)).astype(jnp.bfloat16)
    sent = []
    for k in range(1, MERGE):
        gsend[k, 0:fcols] = gacc[0, k].astype(gsend.dtype)
        gsend[k, fcols:2 * fcols] = gacc[1, k].astype(gsend.dtype)
        gsend[k, 2 * fcols:2 * fcols + 16] = tag
        sent.append(remote(gsend.at[k], grecv.at[k], g_sems, (k,), inner_peer(k)))
    total_s = gacc[0, 0]
    total_n = gacc[1, 0]
    total_b = jnp.where(row_id == 0, colsum, 0.0)
    for k in range(1, MERGE):
        sent[k - 1].wait_recv()
        total_s = total_s + grecv[k, 0:fcols].astype(jnp.float32)
        total_n = total_n + grecv[k, fcols:2 * fcols].astype(jnp.float32)
        total_b = total_b + grecv[k, 2 * fcols:2 * fcols + 16].astype(jnp.float32)
    pending += sent
    vsend[0:fcols] = total_s
    vsend[fcols:2 * fcols] = total_n
    vsend[2 * fcols:2 * fcols + 16] = total_b
    sent = [remote(vsend, vrecv.at[j], v_sems, (j,), group_peer(j)) for j in range(1, groups)]
    for j in range(1, groups):
        sent[j - 1].wait_recv()
        total_s = total_s + vrecv[j, 0:fcols]
        total_n = total_n + vrecv[j, fcols:2 * fcols]
        total_b = total_b + vrecv[j, 2 * fcols:2 * fcols + 16]
    pending += sent
    gs_ref[...] = total_s
    gn_ref[...] = total_n
    gb_ref[...] = jnp.sum(total_b, axis=0, keepdims=True)
    for copy in pending:
        copy.wait_send()


def exchange(feats, aggregated, w_self, w_neigh, bias, upstream):
    groups = lax.axis_size("vgroup")
    nfeat = lax.axis_size("feat")
    outer = nfeat // MERGE
    fcols, width = w_self.shape
    rows = upstream.shape[0]
    any_spec = pl.BlockSpec(memory_space=pl.ANY)
    vmem_spec = pl.BlockSpec(memory_space=pltpu.VMEM)
    dma = pltpu.SemaphoreType.DMA
    return pl.pallas_call(
        functools.partial(exchange_kernel, groups, nfeat),
        out_shape=(
            jax.ShapeDtypeStruct((rows, width), jnp.bfloat16),
            jax.ShapeDtypeStruct((fcols, width), jnp.float32),
            jax.ShapeDtypeStruct((fcols, width), jnp.float32),
            jax.ShapeDtypeStruct((1, width), jnp.float32),
        ),
        in_specs=[any_spec] * 4 + [vmem_spec] * 2,
        out_specs=(vmem_spec,) * 4,
        scratch_shapes=[
            pltpu.VMEM((outer, MERGE, fcols, rows), jnp.bfloat16),
            pltpu.VMEM((outer, MERGE, fcols, rows), jnp.bfloat16),
            pltpu.VMEM((2, MERGE, fcols, width), jnp.bfloat16),
            pltpu.VMEM((outer, rows, width), jnp.bfloat16),
            pltpu.VMEM((outer, rows, width), jnp.bfloat16),
            pltpu.VMEM((outer, rows, width), jnp.bfloat16),
            pltpu.VMEM((2, MERGE, fcols, width), jnp.float32),
            pltpu.VMEM((MERGE, 2 * fcols + 16, width), jnp.bfloat16),
            pltpu.VMEM((MERGE, 2 * fcols + 16, width), jnp.bfloat16),
            pltpu.VMEM((2 * fcols + 16, width), jnp.float32),
            pltpu.VMEM((groups, 2 * fcols + 16, width), jnp.float32),
            dma((2, outer, MERGE)),
            dma((2, outer, MERGE)),
            dma((2, 2, MERGE)),
            dma((2, outer)),
            dma((2, outer)),
            dma((2, MERGE)),
            dma((2, groups)),
            dma((1 + outer, 2)),
        ],
        compiler_params=pltpu.CompilerParams(
            collective_id=0, has_side_effects=True, vmem_limit_bytes=40 * 2**20),
        name="exchange",
    )(feats, aggregated, w_self, w_neigh, bias.reshape(1, width), upstream)


def body(
    features_t, tile_weights, tile_dst, tile_src, tile_count, w_self, w_neigh, bias, grad_hidden
):
    feats = features_t[0]
    ndst = grad_hidden.shape[0] * lax.axis_size("feat")
    aggregated = aggregate(feats, tile_weights[0], tile_dst[0], tile_src[0], tile_count, ndst)
    hidden, grad_self, grad_neigh, grad_bias = exchange(
        feats, aggregated, w_self, w_neigh, bias, grad_hidden)
    return (hidden, grad_self, grad_neigh, grad_bias[0])


def solution(mesh):
    return jax.shard_map(
        body,
        mesh=mesh,
        in_specs=(
            P("vgroup", "feat", None),
            P("vgroup", None, None, None),
            P("vgroup", None),
            P("vgroup", None),
            P("vgroup"),
            P("feat", None),
            P("feat", None),
            P(),
            P(("vgroup", "feat"), None),
        ),
        out_specs=(P(("vgroup", "feat"), None), P("feat", None), P("feat", None), P()),
        check_vma=False,
    )
```

```python
import functools

import jax
import jax.numpy as jnp
from jax import lax
from jax.experimental import pallas as pl
from jax.experimental.pallas import tpu as pltpu
from jax.sharding import PartitionSpec as P

STEP = 64
HALF = 16


def aggregate_kernel(dst_ref, src_ref, count_ref, x_ref, w_ref, out_ref, acc_a, acc_b, buf_a, buf_b):
    step = pl.program_id(0)
    tile = w_ref.shape[1]
    dtiles = out_ref.shape[1] // tile
    base = step * STEP

    @pl.when(step == 0)
    def _():
        acc_a[...] = jnp.zeros_like(acc_a)
        acc_b[...] = jnp.zeros_like(acc_b)
        buf_b[...] = jnp.zeros_like(buf_b)

    def multiply(first, buf):
        for k in range(HALF):
            s = pl.multiple_of(src_ref[base + first + k] * tile, tile)
            buf[k] = lax.dot_general(
                x_ref[:, pl.ds(s, tile)], w_ref[first + k], (((1,), (1,)), ((), ())),
                preferred_element_type=jnp.float32,
            )

    def add(first, buf):
        for k in range(HALF):
            t = first + k
            live = jnp.logical_and(t >= 0, t < count_ref[0])
            d = jnp.where(live, dst_ref[jnp.maximum(t, 0)], dtiles)
            acc = (acc_a, acc_b)[k % 2]
            acc[d] = acc[d] + buf[k]

    @pl.loop(0, STEP // (2 * HALF))
    def _(pair):
        first = pair * 2 * HALF
        multiply(first, buf_a)
        add(base + first - HALF, buf_b)
        multiply(first + HALF, buf_b)
        add(base + first, buf_a)

    @pl.when(step == pl.num_programs(0) - 1)
    def _():
        add(base + STEP - HALF, buf_b)
        for d in range(dtiles):
            out_ref[:, d * tile:(d + 1) * tile] = (acc_a[d] + acc_b[d]).astype(out_ref.dtype)


def aggregate(feats, tiles, dsts, srcs, count, ndst):
    fcols, nsrc = feats.shape
    total, tile, _ = tiles.shape
    return pl.pallas_call(
        aggregate_kernel,
        grid_spec=pltpu.PrefetchScalarGridSpec(
            num_scalar_prefetch=3,
            grid=(total // STEP,),
            in_specs=[
                pl.BlockSpec((fcols, nsrc), lambda i, *_: (0, 0), pipeline_mode=pl.Buffered(1)),
                pl.BlockSpec((STEP, tile, tile), lambda i, *_: (i, 0, 0)),
            ],
            out_specs=pl.BlockSpec((fcols, ndst), lambda i, *_: (0, 0), pipeline_mode=pl.Buffered(1)),
            scratch_shapes=[pltpu.VMEM((ndst // tile + 1, fcols, tile), jnp.float32)] * 2
            + [pltpu.VMEM((HALF, fcols, tile), jnp.float32)] * 2,
        ),
        out_shape=jax.ShapeDtypeStruct((fcols, ndst), jnp.bfloat16),
        compiler_params=pltpu.CompilerParams(vmem_limit_bytes=40 * 2**20),
        cost_estimate=pl.CostEstimate(
            flops=2 * total * fcols * tile * tile, bytes_accessed=total * tile * tile * 2,
            transcendentals=0,
        ),
        name="aggregate",
    )(dsts, srcs, count, feats, tiles)


MERGE = 8
CUBIC = 0.044715
ROOT = 0.7978845608


def arrange_kernel(outer, x_ref, ws_ref, wn_ref, *refs):
    outs, sems = refs[:MERGE // 2], refs[MERGE // 2]
    fcols, width = ws_ref.shape
    rows = outs[0].shape[1]
    me = lax.axis_index("feat")
    copies = []
    for p, out in enumerate(outs):
        for side in range(2):
            for j in range(outer):
                owner = me ^ (j * MERGE + 2 * p + side)
                columns = pl.ds(pl.multiple_of(owner * rows, rows), rows)
                place = side * outer + j
                copies.append(pltpu.make_async_copy(
                    x_ref.at[:, columns], out.at[pl.ds(place * fcols, fcols)], sems.at[p, place]))
        for i, weights in enumerate((ws_ref, wn_ref)):
            copies.append(pltpu.make_async_copy(
                weights, out.at[pl.ds(2 * outer * fcols, fcols), pl.ds(i * width, width)],
                sems.at[p, 2 * outer + i]))
    for copy in copies:
        copy.start()
    for copy in copies:
        copy.wait()


def arrange(feats, w_self, w_neigh, rows):
    outer = lax.axis_size("feat") // MERGE
    fcols, width = w_self.shape
    any_spec = pl.BlockSpec(memory_space=pl.ANY)
    pieces = pl.pallas_call(
        functools.partial(arrange_kernel, outer),
        out_shape=(jax.ShapeDtypeStruct(((2 * outer + 1) * fcols, rows), jnp.bfloat16),) * (MERGE // 2),
        in_specs=[any_spec] * 3,
        out_specs=(any_spec,) * (MERGE // 2),
        scratch_shapes=[pltpu.SemaphoreType.DMA((MERGE // 2, 2 * outer + 2))],
        name="arrange",
    )(feats, w_self, w_neigh)
    nfeat = lax.axis_size("feat")
    moved = [pieces[0]]
    for p in range(1, MERGE // 2):
        moved.append(lax.ppermute(pieces[p], "feat", [(f, f ^ (2 * p)) for f in range(nfeat)]))
    return moved


def exchange_kernel(
    groups, nfeat,
    *refs,
):
    moved, refs = refs[:MERGE // 2], refs[MERGE // 2:]
    a_ref, bias_ref, up_ref, hidden_ref, gs_ref, gn_ref, gb_ref, *refs = refs
    xm, am, wm, psend, precv, dall, gacc, gsend, grecv, vsend, vrecv, *refs = refs
    a_sems, s_sems, p_sems, d_sems, g_sems, v_sems, l_sems, own_sems = refs
    outer = nfeat // MERGE
    fcols = a_ref.shape[0]
    rows = up_ref.shape[0]
    width = up_ref.shape[1]
    grp = lax.axis_index("vgroup")
    me = lax.axis_index("feat")
    lo = lax.rem(me, MERGE)
    hi = lax.div(me, MERGE)

    def inner_peer(k):
        return (grp, hi * MERGE + (lo ^ k))

    def outer_peer(j):
        return (grp, (hi ^ j) * MERGE + lo)

    def group_peer(j):
        return (grp ^ j, me)

    peers = [inner_peer(k) for k in range(1, MERGE)]
    peers += [outer_peer(j) for j in range(1, outer)]
    peers += [group_peer(j) for j in range(1, groups)]
    barrier = pltpu.get_barrier_semaphore()
    for peer in peers:
        pl.semaphore_signal(barrier, inc=1, device_id=peer, device_id_type=pl.DeviceIdType.MESH)
    pl.semaphore_wait(barrier, len(peers))

    def remote(source, target, sems, index, peer):
        copy = pltpu.make_async_remote_copy(
            src_ref=source, dst_ref=target,
            send_sem=sems.at[(0,) + index], recv_sem=sems.at[(1,) + index],
            device_id=peer, device_id_type=pl.DeviceIdType.MESH,
        )
        copy.start()
        return copy

    def columns(j, k):
        owner = (hi ^ j) * MERGE + (lo ^ k)
        return pl.ds(pl.multiple_of(owner * rows, rows), rows)

    order = list(range(1, outer)) + [0]
    pending = []
    local = []
    got = {}
    for j in order:
        got[j] = [
            remote(a_ref.at[:, columns(j, k)], am.at[j, k], a_sems, (j, k), inner_peer(k))
            for k in range(1, MERGE)
        ]
    for j in order:
        local.append(pltpu.make_async_copy(a_ref.at[:, columns(j, 0)], am.at[j, 0], own_sems.at[j]))
    shared = []
    for p, piece in enumerate(moved):
        k = 2 * p
        for j in range(outer):
            local.append(pltpu.make_async_copy(
                piece.at[pl.ds(j * fcols, fcols)], xm.at[j, k], l_sems.at[p, j]))
            shared.append(remote(
                piece.at[pl.ds((outer + j) * fcols, fcols)], xm.at[j, k + 1],
                s_sems, (p, j), inner_peer(1)))
        for i in range(2):
            weights = piece.at[pl.ds(2 * outer * fcols, fcols), pl.ds(i * width, width)]
            local.append(pltpu.make_async_copy(weights, wm.at[i, k], l_sems.at[p, outer + i]))
            shared.append(remote(weights, wm.at[i, k + 1], s_sems, (p, outer + i), inner_peer(1)))
    for copy in local:
        copy.start()
    for copy in local:
        copy.wait()
    for copy in shared:
        copy.wait_recv()
    pending += shared

    merged_cols = MERGE * fcols

    def partial_pre(j):
        total = lax.dot_general(
            xm[j].reshape(merged_cols, rows), wm[0].reshape(merged_cols, width),
            (((0,), (0,)), ((), ())), preferred_element_type=jnp.float32)
        for copy in got[j]:
            copy.wait_recv()
        pending.extend(got[j])
        return total + lax.dot_general(
            am[j].reshape(merged_cols, rows), wm[1].reshape(merged_cols, width),
            (((0,), (0,)), ((), ())), preferred_element_type=jnp.float32)

    sent = []
    for j in range(1, outer):
        psend[j] = partial_pre(j).astype(psend.dtype)
        sent.append(remote(psend.at[j], precv.at[j], p_sems, (j,), outer_peer(j)))
    pre = partial_pre(0) + bias_ref[...]
    for j in range(1, outer):
        sent[j - 1].wait_recv()
        pre = pre + precv[j].astype(jnp.float32)
    pending += sent
    square = pre * pre
    t = jnp.tanh(ROOT * pre * (1.0 + CUBIC * square))
    half = 0.5 * (1.0 + t)
    hidden_ref[...] = (pre * half).astype(hidden_ref.dtype)
    slope = half + 0.5 * pre * (1.0 - t * t) * (ROOT * (1.0 + 3.0 * CUBIC * square))
    dall[0] = (slope * up_ref[...].astype(jnp.float32)).astype(dall.dtype)
    sent = [remote(dall.at[0], dall.at[j], d_sems, (j,), outer_peer(j)) for j in range(1, outer)]

    colsum = jnp.zeros((1, width), jnp.float32)
    for j in range(outer):
        if j > 0:
            sent[j - 1].wait_recv()
        delta = dall[j]
        colsum = colsum + jnp.sum(delta.astype(jnp.float32), axis=0, keepdims=True)
        for i, merged in enumerate((xm, am)):
            part = jnp.dot(
                merged[j].reshape(merged_cols, rows), delta, preferred_element_type=jnp.float32
            ).reshape(MERGE, fcols, width)
            if j == 0:
                gacc[i] = part
            else:
                gacc[i] = gacc[i] + part
    pending += sent
    high = colsum.astype(jnp.bfloat16)
    low = (colsum - high.astype(jnp.float32)).astype(jnp.bfloat16)
    row_id = lax.broadcasted_iota(jnp.int32, (16, width), 0)
    tag = jnp.where(
        row_id == 0, high.astype(jnp.float32),
        jnp.where(row_id == 1, low.astype(jnp.float32), 0.0)).astype(jnp.bfloat16)
    sent = []
    for k in range(1, MERGE):
        gsend[k, 0:fcols] = gacc[0, k].astype(gsend.dtype)
        gsend[k, fcols:2 * fcols] = gacc[1, k].astype(gsend.dtype)
        gsend[k, 2 * fcols:2 * fcols + 16] = tag
        sent.append(remote(gsend.at[k], grecv.at[k], g_sems, (k,), inner_peer(k)))
    total_s = gacc[0, 0]
    total_n = gacc[1, 0]
    total_b = jnp.where(row_id == 0, colsum, 0.0)
    for k in range(1, MERGE):
        sent[k - 1].wait_recv()
        total_s = total_s + grecv[k, 0:fcols].astype(jnp.float32)
        total_n = total_n + grecv[k, fcols:2 * fcols].astype(jnp.float32)
        total_b = total_b + grecv[k, 2 * fcols:2 * fcols + 16].astype(jnp.float32)
    pending += sent
    vsend[0:fcols] = total_s
    vsend[fcols:2 * fcols] = total_n
    vsend[2 * fcols:2 * fcols + 16] = total_b
    sent = [remote(vsend, vrecv.at[j], v_sems, (j,), group_peer(j)) for j in range(1, groups)]
    for j in range(1, groups):
        sent[j - 1].wait_recv()
        total_s = total_s + vrecv[j, 0:fcols]
        total_n = total_n + vrecv[j, fcols:2 * fcols]
        total_b = total_b + vrecv[j, 2 * fcols:2 * fcols + 16]
    pending += sent
    gs_ref[...] = total_s
    gn_ref[...] = total_n
    gb_ref[...] = jnp.sum(total_b, axis=0, keepdims=True)
    for copy in pending:
        copy.wait_send()


def exchange(moved, aggregated, bias, upstream):
    groups = lax.axis_size("vgroup")
    nfeat = lax.axis_size("feat")
    outer = nfeat // MERGE
    fcols = aggregated.shape[0]
    rows, width = upstream.shape
    any_spec = pl.BlockSpec(memory_space=pl.ANY)
    vmem_spec = pl.BlockSpec(memory_space=pltpu.VMEM)
    dma = pltpu.SemaphoreType.DMA
    return pl.pallas_call(
        functools.partial(exchange_kernel, groups, nfeat),
        out_shape=(
            jax.ShapeDtypeStruct((rows, width), jnp.bfloat16),
            jax.ShapeDtypeStruct((fcols, width), jnp.float32),
            jax.ShapeDtypeStruct((fcols, width), jnp.float32),
            jax.ShapeDtypeStruct((1, width), jnp.float32),
        ),
        in_specs=[any_spec] * (MERGE // 2 + 1) + [vmem_spec] * 2,
        out_specs=(vmem_spec,) * 4,
        scratch_shapes=[
            pltpu.VMEM((outer, MERGE, fcols, rows), jnp.bfloat16),
            pltpu.VMEM((outer, MERGE, fcols, rows), jnp.bfloat16),
            pltpu.VMEM((2, MERGE, fcols, width), jnp.bfloat16),
            pltpu.VMEM((outer, rows, width), jnp.bfloat16),
            pltpu.VMEM((outer, rows, width), jnp.bfloat16),
            pltpu.VMEM((outer, rows, width), jnp.bfloat16),
            pltpu.VMEM((2, MERGE, fcols, width), jnp.float32),
            pltpu.VMEM((MERGE, 2 * fcols + 16, width), jnp.bfloat16),
            pltpu.VMEM((MERGE, 2 * fcols + 16, width), jnp.bfloat16),
            pltpu.VMEM((2 * fcols + 16, width), jnp.float32),
            pltpu.VMEM((groups, 2 * fcols + 16, width), jnp.float32),
            dma((2, outer, MERGE)),
            dma((2, MERGE // 2, outer + 2)),
            dma((2, outer)),
            dma((2, outer)),
            dma((2, MERGE)),
            dma((2, groups)),
            dma((MERGE // 2, outer + 2)),
            dma((outer,)),
        ],
        compiler_params=pltpu.CompilerParams(
            collective_id=0, has_side_effects=True, vmem_limit_bytes=40 * 2**20),
        name="exchange",
    )(*moved, aggregated, bias.reshape(1, width), upstream)


def body(
    features_t, tile_weights, tile_dst, tile_src, tile_count, w_self, w_neigh, bias, grad_hidden
):
    feats = features_t[0]
    ndst = grad_hidden.shape[0] * lax.axis_size("feat")
    moved = arrange(feats, w_self, w_neigh, grad_hidden.shape[0])
    aggregated = aggregate(feats, tile_weights[0], tile_dst[0], tile_src[0], tile_count, ndst)
    hidden, grad_self, grad_neigh, grad_bias = exchange(moved, aggregated, bias, grad_hidden)
    return (hidden, grad_self, grad_neigh, grad_bias[0])


def solution(mesh):
    return jax.shard_map(
        body,
        mesh=mesh,
        in_specs=(
            P("vgroup", "feat", None),
            P("vgroup", None, None, None),
            P("vgroup", None),
            P("vgroup", None),
            P("vgroup"),
            P("feat", None),
            P("feat", None),
            P(),
            P(("vgroup", "feat"), None),
        ),
        out_specs=(P(("vgroup", "feat"), None), P("feat", None), P("feat", None), P()),
        check_vma=False,
    )
```

```python
import functools

import jax
import jax.numpy as jnp
from jax import lax
from jax.experimental import pallas as pl
from jax.experimental.pallas import tpu as pltpu
from jax.sharding import PartitionSpec as P

STEP = 64
HALF = 16


def aggregate_kernel(dst_ref, src_ref, count_ref, x_ref, w_ref, out_ref, acc_a, acc_b, buf_a, buf_b):
    step = pl.program_id(0)
    tile = w_ref.shape[1]
    dtiles = out_ref.shape[1] // tile
    base = step * STEP

    @pl.when(step == 0)
    def _():
        acc_a[...] = jnp.zeros_like(acc_a)
        acc_b[...] = jnp.zeros_like(acc_b)
        buf_b[...] = jnp.zeros_like(buf_b)

    def multiply(first, buf):
        for k in range(0, HALF, 2):
            one, two = [
                x_ref[:, pl.ds(pl.multiple_of(src_ref[base + first + k + n] * tile, tile), tile)]
                for n in range(2)
            ]
            zero = jnp.zeros_like(one)
            left = jnp.concatenate([
                jnp.concatenate([one, zero], axis=1), jnp.concatenate([zero, two], axis=1)], axis=0)
            right = jnp.concatenate([w_ref[first + k], w_ref[first + k + 1]], axis=1)
            prod = lax.dot_general(
                left, right, (((1,), (1,)), ((), ())), preferred_element_type=jnp.float32)
            buf[k] = prod[:one.shape[0]]
            buf[k + 1] = prod[one.shape[0]:]

    def add(first, buf):
        for k in range(HALF):
            t = first + k
            live = jnp.logical_and(t >= 0, t < count_ref[0])
            d = jnp.where(live, dst_ref[jnp.maximum(t, 0)], dtiles)
            acc = (acc_a, acc_b)[k % 2]
            acc[d] = acc[d] + buf[k]

    @pl.loop(0, STEP // (2 * HALF))
    def _(pair):
        first = pair * 2 * HALF
        multiply(first, buf_a)
        add(base + first - HALF, buf_b)
        multiply(first + HALF, buf_b)
        add(base + first, buf_a)

    @pl.when(step == pl.num_programs(0) - 1)
    def _():
        add(base + STEP - HALF, buf_b)
        for d in range(dtiles):
            out_ref[:, d * tile:(d + 1) * tile] = (acc_a[d] + acc_b[d]).astype(out_ref.dtype)


def aggregate(feats, tiles, dsts, srcs, count, ndst):
    fcols, nsrc = feats.shape
    total, tile, _ = tiles.shape
    return pl.pallas_call(
        aggregate_kernel,
        grid_spec=pltpu.PrefetchScalarGridSpec(
            num_scalar_prefetch=3,
            grid=(total // STEP,),
            in_specs=[
                pl.BlockSpec((fcols, nsrc), lambda i, *_: (0, 0), pipeline_mode=pl.Buffered(1)),
                pl.BlockSpec((STEP, tile, tile), lambda i, *_: (i, 0, 0)),
            ],
            out_specs=pl.BlockSpec((fcols, ndst), lambda i, *_: (0, 0), pipeline_mode=pl.Buffered(1)),
            scratch_shapes=[pltpu.VMEM((ndst // tile + 1, fcols, tile), jnp.float32)] * 2
            + [pltpu.VMEM((HALF, fcols, tile), jnp.float32)] * 2,
        ),
        out_shape=jax.ShapeDtypeStruct((fcols, ndst), jnp.bfloat16),
        compiler_params=pltpu.CompilerParams(vmem_limit_bytes=40 * 2**20),
        cost_estimate=pl.CostEstimate(
            flops=2 * total * fcols * tile * tile, bytes_accessed=total * tile * tile * 2,
            transcendentals=0,
        ),
        name="aggregate",
    )(dsts, srcs, count, feats, tiles)


MERGE = 8
PARTS = 2
CUBIC = 0.044715
ROOT = 0.7978845608


def arrange_kernel(outer, x_ref, ws_ref, wn_ref, *refs):
    outs = refs
    fcols, width = ws_ref.shape
    rows = outs[0].shape[1]
    me = lax.axis_index("feat")
    for p, out in enumerate(outs):
        for side in range(2):
            for j in range(outer):
                owner = me ^ (j * MERGE + 2 * p + side)
                columns = pl.ds(pl.multiple_of(owner * rows, rows), rows)
                place = side * outer + j
                out[place * fcols:(place + 1) * fcols] = x_ref[:, columns]
        last = slice(2 * outer * fcols, (2 * outer + 1) * fcols)
        out[last, 0:width] = ws_ref[...]
        out[last, width:2 * width] = wn_ref[...]


def arrange(feats, w_self, w_neigh, rows):
    outer = lax.axis_size("feat") // MERGE
    fcols, width = w_self.shape
    nfeat = lax.axis_size("feat")
    pieces = pl.pallas_call(
        functools.partial(arrange_kernel, outer),
        out_shape=(jax.ShapeDtypeStruct(((2 * outer + 1) * fcols, rows), jnp.bfloat16),) * (MERGE // 2),
        grid=(1,),
        in_specs=[
            pl.BlockSpec((fcols, rows * nfeat), lambda i: (0, 0)),
            pl.BlockSpec((fcols, width), lambda i: (0, 0)),
            pl.BlockSpec((fcols, width), lambda i: (0, 0)),
        ],
        out_specs=(pl.BlockSpec(((2 * outer + 1) * fcols, rows), lambda i: (0, 0)),) * (MERGE // 2),
        compiler_params=pltpu.CompilerParams(vmem_limit_bytes=24 * 2**20),
        name="arrange",
    )(feats, w_self, w_neigh)
    moved = [pieces[0]]
    for p in range(1, MERGE // 2):
        moved.append(lax.ppermute(pieces[p], "feat", [(f, f ^ (2 * p)) for f in range(nfeat)]))
    return moved


def exchange_kernel(
    groups, nfeat,
    *refs,
):
    moved, refs = refs[:MERGE // 2], refs[MERGE // 2:]
    a_ref, bias_ref, up_ref, hidden_ref, gs_ref, gn_ref, gb_ref, *refs = refs
    xm, am, wm, psend, precv, dall, gacc, gsend, grecv, vsend, vrecv, *refs = refs
    a_sems, s_sems, p_sems, d_sems, g_sems, v_sems, l_sems, own_sems = refs
    outer = nfeat // MERGE
    fcols = a_ref.shape[0]
    rows = up_ref.shape[0]
    width = up_ref.shape[1]
    grp = lax.axis_index("vgroup")
    me = lax.axis_index("feat")
    lo = lax.rem(me, MERGE)
    hi = lax.div(me, MERGE)

    def inner_peer(k):
        return (grp, hi * MERGE + (lo ^ k))

    def outer_peer(j):
        return (grp, (hi ^ j) * MERGE + lo)

    def group_peer(j):
        return (grp ^ j, me)

    peers = [inner_peer(k) for k in range(1, MERGE)]
    peers += [outer_peer(j) for j in range(1, outer)]
    peers += [group_peer(j) for j in range(1, groups)]
    barrier = pltpu.get_barrier_semaphore()
    for peer in peers:
        pl.semaphore_signal(barrier, inc=1, device_id=peer, device_id_type=pl.DeviceIdType.MESH)
    pl.semaphore_wait(barrier, len(peers))

    def remote(source, target, sems, index, peer):
        copy = pltpu.make_async_remote_copy(
            src_ref=source, dst_ref=target,
            send_sem=sems.at[(0,) + index], recv_sem=sems.at[(1,) + index],
            device_id=peer, device_id_type=pl.DeviceIdType.MESH,
        )
        copy.start()
        return copy

    def columns(j, k):
        owner = (hi ^ j) * MERGE + (lo ^ k)
        return pl.ds(pl.multiple_of(owner * rows, rows), rows)

    order = list(range(1, outer)) + [0]
    pending = []
    local = []
    got = {}
    for j in order:
        got[j] = [
            remote(a_ref.at[:, columns(j, k)], am.at[j, k], a_sems, (j, k), inner_peer(k))
            for k in range(1, MERGE)
        ]
    for j in order:
        local.append(pltpu.make_async_copy(a_ref.at[:, columns(j, 0)], am.at[j, 0], own_sems.at[j]))
    shared = []
    for p, piece in enumerate(moved):
        k = 2 * p
        for j in range(outer):
            local.append(pltpu.make_async_copy(
                piece.at[pl.ds(j * fcols, fcols)], xm.at[j, k], l_sems.at[p, j]))
            shared.append(remote(
                piece.at[pl.ds((outer + j) * fcols, fcols)], xm.at[j, k + 1],
                s_sems, (p, j), inner_peer(1)))
        for i in range(2):
            weights = piece.at[pl.ds(2 * outer * fcols, fcols), pl.ds(i * width, width)]
            local.append(pltpu.make_async_copy(weights, wm.at[i, k], l_sems.at[p, outer + i]))
            shared.append(remote(weights, wm.at[i, k + 1], s_sems, (p, outer + i), inner_peer(1)))
    for copy in local:
        copy.start()
    for copy in local:
        copy.wait()
    for copy in shared:
        copy.wait_recv()
    pending += shared

    merged_cols = MERGE * fcols

    part_rows = rows // PARTS

    def partial_pre(j, c):
        span = slice(c * part_rows, (c + 1) * part_rows)
        total = lax.dot_general(
            xm[j, :, :, span].reshape(merged_cols, part_rows), wm[0].reshape(merged_cols, width),
            (((0,), (0,)), ((), ())), preferred_element_type=jnp.float32)
        if c == 0:
            for copy in got[j]:
                copy.wait_recv()
            pending.extend(got[j])
        return total + lax.dot_general(
            am[j, :, :, span].reshape(merged_cols, part_rows), wm[1].reshape(merged_cols, width),
            (((0,), (0,)), ((), ())), preferred_element_type=jnp.float32)

    def grads(j, c, colsum):
        span = slice(c * part_rows, (c + 1) * part_rows)
        delta = dall[j, span]
        for i, merged in enumerate((xm, am)):
            part = jnp.dot(
                merged[j, :, :, span].reshape(merged_cols, part_rows), delta,
                preferred_element_type=jnp.float32,
            ).reshape(MERGE, fcols, width)
            if j == 0 and c == 0:
                gacc[i] = part
            else:
                gacc[i] = gacc[i] + part
        return colsum + jnp.sum(delta.astype(jnp.float32), axis=0, keepdims=True)

    sent = {}
    for c in range(PARTS):
        span = pl.ds(c * part_rows, part_rows)
        for j in range(1, outer):
            psend[j, span] = partial_pre(j, c).astype(psend.dtype)
            sent[j, c] = remote(
                psend.at[j, span], precv.at[j, span], p_sems, (j, c), outer_peer(j))
    deltas = {}
    for c in range(PARTS):
        span = pl.ds(c * part_rows, part_rows)
        pre = partial_pre(0, c) + bias_ref[...]
        for j in range(1, outer):
            sent[j, c].wait_recv()
            pre = pre + precv[j, span].astype(jnp.float32)
        square = pre * pre
        t = jnp.tanh(ROOT * pre * (1.0 + CUBIC * square))
        half = 0.5 * (1.0 + t)
        slope = half + 0.5 * pre * (1.0 - t * t) * (ROOT * (1.0 + 3.0 * CUBIC * square))
        dall[0, span] = (slope * up_ref[span].astype(jnp.float32)).astype(dall.dtype)
        for j in range(1, outer):
            deltas[j, c] = remote(
                dall.at[0, span], dall.at[j, span], d_sems, (j, c), outer_peer(j))
        hidden_ref[span] = (pre * half).astype(hidden_ref.dtype)
    pending += list(sent.values())
    pending += list(deltas.values())

    colsum = jnp.zeros((1, width), jnp.float32)
    for c in range(PARTS):
        colsum = grads(0, c, colsum)
    for c in range(PARTS):
        for j in range(1, outer):
            deltas[j, c].wait_recv()
            colsum = grads(j, c, colsum)
    high = colsum.astype(jnp.bfloat16)
    low = (colsum - high.astype(jnp.float32)).astype(jnp.bfloat16)
    row_id = lax.broadcasted_iota(jnp.int32, (16, width), 0)
    tag = jnp.where(
        row_id == 0, high.astype(jnp.float32),
        jnp.where(row_id == 1, low.astype(jnp.float32), 0.0)).astype(jnp.bfloat16)
    sent = []
    for k in range(1, MERGE):
        gsend[k, 0:fcols] = gacc[0, k].astype(gsend.dtype)
        gsend[k, fcols:2 * fcols] = gacc[1, k].astype(gsend.dtype)
        gsend[k, 2 * fcols:2 * fcols + 16] = tag
        sent.append(remote(gsend.at[k], grecv.at[k], g_sems, (k,), inner_peer(k)))
    total_s = gacc[0, 0]
    total_n = gacc[1, 0]
    total_b = jnp.where(row_id == 0, colsum, 0.0)
    for k in range(1, MERGE):
        sent[k - 1].wait_recv()
        total_s = total_s + grecv[k, 0:fcols].astype(jnp.float32)
        total_n = total_n + grecv[k, fcols:2 * fcols].astype(jnp.float32)
        total_b = total_b + grecv[k, 2 * fcols:2 * fcols + 16].astype(jnp.float32)
    pending += sent
    vsend[0:fcols] = total_s
    vsend[fcols:2 * fcols] = total_n
    vsend[2 * fcols:2 * fcols + 16] = total_b
    sent = [remote(vsend, vrecv.at[j], v_sems, (j,), group_peer(j)) for j in range(1, groups)]
    for j in range(1, groups):
        sent[j - 1].wait_recv()
        total_s = total_s + vrecv[j, 0:fcols]
        total_n = total_n + vrecv[j, fcols:2 * fcols]
        total_b = total_b + vrecv[j, 2 * fcols:2 * fcols + 16]
    pending += sent
    gs_ref[...] = total_s
    gn_ref[...] = total_n
    gb_ref[...] = jnp.sum(total_b, axis=0, keepdims=True)
    for copy in pending:
        copy.wait_send()


def exchange(moved, aggregated, bias, upstream):
    groups = lax.axis_size("vgroup")
    nfeat = lax.axis_size("feat")
    outer = nfeat // MERGE
    fcols = aggregated.shape[0]
    rows, width = upstream.shape
    any_spec = pl.BlockSpec(memory_space=pl.ANY)
    vmem_spec = pl.BlockSpec(memory_space=pltpu.VMEM)
    dma = pltpu.SemaphoreType.DMA
    return pl.pallas_call(
        functools.partial(exchange_kernel, groups, nfeat),
        out_shape=(
            jax.ShapeDtypeStruct((rows, width), jnp.bfloat16),
            jax.ShapeDtypeStruct((fcols, width), jnp.float32),
            jax.ShapeDtypeStruct((fcols, width), jnp.float32),
            jax.ShapeDtypeStruct((1, width), jnp.float32),
        ),
        in_specs=[any_spec] * (MERGE // 2 + 1) + [vmem_spec] * 2,
        out_specs=(vmem_spec,) * 4,
        scratch_shapes=[
            pltpu.VMEM((outer, MERGE, fcols, rows), jnp.bfloat16),
            pltpu.VMEM((outer, MERGE, fcols, rows), jnp.bfloat16),
            pltpu.VMEM((2, MERGE, fcols, width), jnp.bfloat16),
            pltpu.VMEM((outer, rows, width), jnp.bfloat16),
            pltpu.VMEM((outer, rows, width), jnp.bfloat16),
            pltpu.VMEM((outer, rows, width), jnp.bfloat16),
            pltpu.VMEM((2, MERGE, fcols, width), jnp.float32),
            pltpu.VMEM((MERGE, 2 * fcols + 16, width), jnp.bfloat16),
            pltpu.VMEM((MERGE, 2 * fcols + 16, width), jnp.bfloat16),
            pltpu.VMEM((2 * fcols + 16, width), jnp.float32),
            pltpu.VMEM((groups, 2 * fcols + 16, width), jnp.float32),
            dma((2, outer, MERGE)),
            dma((2, MERGE // 2, outer + 2)),
            dma((2, outer, PARTS)),
            dma((2, outer, PARTS)),
            dma((2, MERGE)),
            dma((2, groups)),
            dma((MERGE // 2, outer + 2)),
            dma((outer,)),
        ],
        compiler_params=pltpu.CompilerParams(
            collective_id=0, has_side_effects=True, vmem_limit_bytes=40 * 2**20),
        name="exchange",
    )(*moved, aggregated, bias.reshape(1, width), upstream)


def body(
    features_t, tile_weights, tile_dst, tile_src, tile_count, w_self, w_neigh, bias, grad_hidden
):
    feats = features_t[0]
    ndst = grad_hidden.shape[0] * lax.axis_size("feat")
    moved = arrange(feats, w_self, w_neigh, grad_hidden.shape[0])
    aggregated = aggregate(feats, tile_weights[0], tile_dst[0], tile_src[0], tile_count, ndst)
    hidden, grad_self, grad_neigh, grad_bias = exchange(moved, aggregated, bias, grad_hidden)
    return (hidden, grad_self, grad_neigh, grad_bias[0])


def solution(mesh):
    return jax.shard_map(
        body,
        mesh=mesh,
        in_specs=(
            P("vgroup", "feat", None),
            P("vgroup", None, None, None),
            P("vgroup", None),
            P("vgroup", None),
            P("vgroup"),
            P("feat", None),
            P("feat", None),
            P(),
            P(("vgroup", "feat"), None),
        ),
        out_specs=(P(("vgroup", "feat"), None), P("feat", None), P("feat", None), P()),
        check_vma=False,
    )
```

```python
import functools

import jax
import jax.numpy as jnp
from jax import lax
from jax.experimental import pallas as pl
from jax.experimental.pallas import tpu as pltpu
from jax.sharding import PartitionSpec as P

STEP = 64
UNROLL = 32


def aggregate_kernel(dst_ref, src_ref, count_ref, x_ref, w_ref, out_ref, acc_a, acc_b):
    step = pl.program_id(0)
    tile = w_ref.shape[1]
    dtiles = out_ref.shape[1] // tile
    base = step * STEP

    @pl.when(step == 0)
    def _():
        acc_a[...] = jnp.zeros_like(acc_a)
        acc_b[...] = jnp.zeros_like(acc_b)

    def place(i):
        t = base + i
        return jnp.where(t < count_ref[0], dst_ref[t], dtiles)

    @pl.loop(0, STEP // UNROLL)
    def _(group):
        for k in range(0, UNROLL, 2):
            i = group * UNROLL + k
            one, two = [
                x_ref[:, pl.ds(pl.multiple_of(src_ref[base + i + n] * tile, tile), tile)]
                for n in range(2)
            ]
            zero = jnp.zeros_like(one)
            left = jnp.concatenate([
                jnp.concatenate([one, zero], axis=1), jnp.concatenate([zero, two], axis=1)], axis=0)
            right = jnp.concatenate([w_ref[i], w_ref[i + 1]], axis=1)
            prod = lax.dot_general(
                left, right, (((1,), (1,)), ((), ())), preferred_element_type=jnp.float32)
            a, b = place(i), place(i + 1)
            acc_a[a] = acc_a[a] + prod[:one.shape[0]]
            acc_b[b] = acc_b[b] + prod[one.shape[0]:]

    @pl.when(step == pl.num_programs(0) - 1)
    def _():
        for d in range(dtiles):
            out_ref[:, d * tile:(d + 1) * tile] = (acc_a[d] + acc_b[d]).astype(out_ref.dtype)


def aggregate(feats, tiles, dsts, srcs, count, ndst):
    fcols, nsrc = feats.shape
    total, tile, _ = tiles.shape
    return pl.pallas_call(
        aggregate_kernel,
        grid_spec=pltpu.PrefetchScalarGridSpec(
            num_scalar_prefetch=3,
            grid=(total // STEP,),
            in_specs=[
                pl.BlockSpec((fcols, nsrc), lambda i, *_: (0, 0), pipeline_mode=pl.Buffered(1)),
                pl.BlockSpec((STEP, tile, tile), lambda i, *_: (i, 0, 0)),
            ],
            out_specs=pl.BlockSpec((fcols, ndst), lambda i, *_: (0, 0), pipeline_mode=pl.Buffered(1)),
            scratch_shapes=[pltpu.VMEM((ndst // tile + 1, fcols, tile), jnp.float32)] * 2,
        ),
        out_shape=jax.ShapeDtypeStruct((fcols, ndst), jnp.bfloat16),
        compiler_params=pltpu.CompilerParams(vmem_limit_bytes=60 * 2**20),
        cost_estimate=pl.CostEstimate(
            flops=2 * total * fcols * tile * tile, bytes_accessed=total * tile * tile * 2,
            transcendentals=0,
        ),
        name="aggregate",
    )(dsts, srcs, count, feats, tiles)


MERGE = 8
PARTS = 2
CUBIC = 0.044715
ROOT = 0.7978845608


def arrange_kernel(outer, x_ref, ws_ref, wn_ref, *refs):
    outs = refs
    fcols, width = ws_ref.shape
    rows = outs[0].shape[1]
    me = lax.axis_index("feat")
    for p, out in enumerate(outs):
        for side in range(2):
            for j in range(outer):
                owner = me ^ (j * MERGE + 2 * p + side)
                columns = pl.ds(pl.multiple_of(owner * rows, rows), rows)
                place = side * outer + j
                out[place * fcols:(place + 1) * fcols] = x_ref[:, columns]
        last = slice(2 * outer * fcols, (2 * outer + 1) * fcols)
        out[last, 0:width] = ws_ref[...]
        out[last, width:2 * width] = wn_ref[...]


def arrange(feats, w_self, w_neigh, rows):
    outer = lax.axis_size("feat") // MERGE
    fcols, width = w_self.shape
    nfeat = lax.axis_size("feat")
    pieces = pl.pallas_call(
        functools.partial(arrange_kernel, outer),
        out_shape=(jax.ShapeDtypeStruct(((2 * outer + 1) * fcols, rows), jnp.bfloat16),) * (MERGE // 2),
        grid=(1,),
        in_specs=[
            pl.BlockSpec((fcols, rows * nfeat), lambda i: (0, 0)),
            pl.BlockSpec((fcols, width), lambda i: (0, 0)),
            pl.BlockSpec((fcols, width), lambda i: (0, 0)),
        ],
        out_specs=(pl.BlockSpec(((2 * outer + 1) * fcols, rows), lambda i: (0, 0)),) * (MERGE // 2),
        compiler_params=pltpu.CompilerParams(vmem_limit_bytes=60 * 2**20),
        name="arrange",
    )(feats, w_self, w_neigh)
    moved = [pieces[0]]
    for p in range(1, MERGE // 2):
        moved.append(lax.ppermute(pieces[p], "feat", [(f, f ^ (2 * p)) for f in range(nfeat)]))
    return moved


def exchange_kernel(
    groups, nfeat,
    *refs,
):
    moved, refs = refs[:MERGE // 2], refs[MERGE // 2:]
    a_ref, bias_ref, up_ref, hidden_ref, gs_ref, gn_ref, gb_ref, *refs = refs
    xm, am, wm, psend, precv, dall, gacc, gsend, gpair, gout, grecv, vsend, vrecv, *refs = refs
    a_sems, s_sems, p_sems, d_sems, h_sems, g_sems, v_sems, l_sems, own_sems = refs
    outer = nfeat // MERGE
    fcols = a_ref.shape[0]
    rows = up_ref.shape[0]
    width = up_ref.shape[1]
    grp = lax.axis_index("vgroup")
    me = lax.axis_index("feat")
    lo = lax.rem(me, MERGE)
    hi = lax.div(me, MERGE)

    def inner_peer(k):
        return (grp, hi * MERGE + (lo ^ k))

    def outer_peer(j):
        return (grp, (hi ^ j) * MERGE + lo)

    def group_peer(j):
        return (grp ^ j, me)

    peers = [inner_peer(k) for k in range(1, MERGE)]
    peers += [outer_peer(j) for j in range(1, outer)]
    peers += [group_peer(j) for j in range(1, groups)]
    barrier = pltpu.get_barrier_semaphore()
    for peer in peers:
        pl.semaphore_signal(barrier, inc=1, device_id=peer, device_id_type=pl.DeviceIdType.MESH)
    pl.semaphore_wait(barrier, len(peers))

    def remote(source, target, sems, index, peer):
        copy = pltpu.make_async_remote_copy(
            src_ref=source, dst_ref=target,
            send_sem=sems.at[(0,) + index], recv_sem=sems.at[(1,) + index],
            device_id=peer, device_id_type=pl.DeviceIdType.MESH,
        )
        copy.start()
        return copy

    def columns(j, k):
        owner = (hi ^ j) * MERGE + (lo ^ k)
        return pl.ds(pl.multiple_of(owner * rows, rows), rows)

    order = list(range(1, outer)) + [0]
    pending = []
    local = []
    got = {}

    def send_columns(j):
        got[j] = [
            remote(a_ref.at[:, columns(j, k)], am.at[j, k], a_sems, (j, k), inner_peer(k))
            for k in range(1, MERGE)
        ]

    send_columns(order[0])
    for j in order:
        local.append(pltpu.make_async_copy(a_ref.at[:, columns(j, 0)], am.at[j, 0], own_sems.at[j]))
    shared = []
    for p, piece in enumerate(moved):
        k = 2 * p
        for j in range(outer):
            local.append(pltpu.make_async_copy(
                piece.at[pl.ds(j * fcols, fcols)], xm.at[j, k], l_sems.at[p, j]))
            shared.append(remote(
                piece.at[pl.ds((outer + j) * fcols, fcols)], xm.at[j, k + 1],
                s_sems, (p, j), inner_peer(1)))
        for i in range(2):
            weights = piece.at[pl.ds(2 * outer * fcols, fcols), pl.ds(i * width, width)]
            local.append(pltpu.make_async_copy(weights, wm.at[i, k], l_sems.at[p, outer + i]))
            shared.append(remote(weights, wm.at[i, k + 1], s_sems, (p, outer + i), inner_peer(1)))
    for copy in local:
        copy.start()
    for copy in local:
        copy.wait()
    for copy in shared:
        copy.wait_recv()
    pending += shared

    merged_cols = MERGE * fcols

    part_rows = rows // PARTS

    def partial_pre(j, c):
        span = slice(c * part_rows, (c + 1) * part_rows)
        total = lax.dot_general(
            xm[j, :, :, span].reshape(merged_cols, part_rows), wm[0].reshape(merged_cols, width),
            (((0,), (0,)), ((), ())), preferred_element_type=jnp.float32)
        if c == 0:
            for copy in got[j]:
                copy.wait_recv()
            pending.extend(got[j])
            if j > 0:
                send_columns(order[order.index(j) + 1])
        return total + lax.dot_general(
            am[j, :, :, span].reshape(merged_cols, part_rows), wm[1].reshape(merged_cols, width),
            (((0,), (0,)), ((), ())), preferred_element_type=jnp.float32)

    def grads(j, c, colsum):
        span = slice(c * part_rows, (c + 1) * part_rows)
        delta = dall[j, span]
        for i, merged in enumerate((xm, am)):
            part = jnp.dot(
                merged[j, :, :, span].reshape(merged_cols, part_rows), delta,
                preferred_element_type=jnp.float32,
            ).reshape(MERGE, fcols, width)
            if j == 0 and c == 0:
                gacc[i] = part
            else:
                gacc[i] = gacc[i] + part
        return colsum + jnp.sum(delta.astype(jnp.float32), axis=0, keepdims=True)

    sent = {}
    for j in range(1, outer):
        for c in range(PARTS):
            span = pl.ds(c * part_rows, part_rows)
            psend[j, span] = partial_pre(j, c).astype(psend.dtype)
            sent[j, c] = remote(
                psend.at[j, span], precv.at[j, span], p_sems, (j, c), outer_peer(j))
    deltas = {}
    for c in range(PARTS):
        span = pl.ds(c * part_rows, part_rows)
        pre = partial_pre(0, c) + bias_ref[...]
        for j in range(1, outer):
            sent[j, c].wait_recv()
            pre = pre + precv[j, span].astype(jnp.float32)
        square = pre * pre
        t = jnp.tanh(ROOT * pre * (1.0 + CUBIC * square))
        half = 0.5 * (1.0 + t)
        slope = half + 0.5 * pre * (1.0 - t * t) * (ROOT * (1.0 + 3.0 * CUBIC * square))
        dall[0, span] = (slope * up_ref[span].astype(jnp.float32)).astype(dall.dtype)
        for j in range(1, outer):
            deltas[j, c] = remote(
                dall.at[0, span], dall.at[j, span], d_sems, (j, c), outer_peer(j))
        hidden_ref[span] = (pre * half).astype(hidden_ref.dtype)
    pending += list(sent.values())
    pending += list(deltas.values())

    colsum = jnp.zeros((1, width), jnp.float32)
    for c in range(PARTS):
        colsum = grads(0, c, colsum)
    for c in range(PARTS):
        for j in range(1, outer):
            deltas[j, c].wait_recv()
            colsum = grads(j, c, colsum)
    row_id = lax.broadcasted_iota(jnp.int32, (16, width), 0)
    tail = slice(2 * fcols, 2 * fcols + 16)

    def split(value):
        high = value.astype(jnp.bfloat16).astype(jnp.float32)
        return jnp.where(
            row_id == 0, high, jnp.where(row_id == 1, value - high, 0.0)).astype(jnp.bfloat16)

    def join(block):
        return jnp.sum(block.astype(jnp.float32), axis=0, keepdims=True)

    tag = split(colsum)
    pairs = MERGE // 2
    sent = {}
    for m in list(range(1, pairs)) + [0]:
        gsend[m, 0:fcols] = gacc[0, 2 * m + 1].astype(gsend.dtype)
        gsend[m, fcols:2 * fcols] = gacc[1, 2 * m + 1].astype(gsend.dtype)
        gsend[m, tail] = tag
        sent[m] = remote(gsend.at[m], gpair.at[m], h_sems, (m,), inner_peer(1))
    passed = {}
    for m in range(1, pairs):
        sent[m].wait_recv()
        if m == 1:
            colsum = colsum + join(gpair[1, tail])
            tag = split(colsum)
        gout[m, 0:fcols] = (gacc[0, 2 * m] + gpair[m, 0:fcols].astype(jnp.float32)).astype(gout.dtype)
        gout[m, fcols:2 * fcols] = (
            gacc[1, 2 * m] + gpair[m, fcols:2 * fcols].astype(jnp.float32)).astype(gout.dtype)
        gout[m, tail] = tag
        passed[m] = remote(gout.at[m], grecv.at[m], g_sems, (m,), inner_peer(2 * m))
    sent[0].wait_recv()
    total_s = gacc[0, 0] + gpair[0, 0:fcols].astype(jnp.float32)
    total_n = gacc[1, 0] + gpair[0, fcols:2 * fcols].astype(jnp.float32)
    for m in range(1, pairs):
        passed[m].wait_recv()
        total_s = total_s + grecv[m, 0:fcols].astype(jnp.float32)
        total_n = total_n + grecv[m, fcols:2 * fcols].astype(jnp.float32)
        colsum = colsum + join(grecv[m, tail])
    total_b = jnp.where(row_id == 0, colsum, 0.0)
    pending += list(sent.values())
    pending += list(passed.values())
    vsend[0:fcols] = total_s
    vsend[fcols:2 * fcols] = total_n
    vsend[2 * fcols:2 * fcols + 16] = total_b
    sent = [remote(vsend, vrecv.at[j], v_sems, (j,), group_peer(j)) for j in range(1, groups)]
    for j in range(1, groups):
        sent[j - 1].wait_recv()
        total_s = total_s + vrecv[j, 0:fcols]
        total_n = total_n + vrecv[j, fcols:2 * fcols]
        total_b = total_b + vrecv[j, 2 * fcols:2 * fcols + 16]
    pending += sent
    gs_ref[...] = total_s
    gn_ref[...] = total_n
    gb_ref[...] = jnp.sum(total_b, axis=0, keepdims=True)
    for copy in pending:
        copy.wait_send()


def exchange(moved, aggregated, bias, upstream):
    groups = lax.axis_size("vgroup")
    nfeat = lax.axis_size("feat")
    outer = nfeat // MERGE
    fcols = aggregated.shape[0]
    rows, width = upstream.shape
    any_spec = pl.BlockSpec(memory_space=pl.ANY)
    vmem_spec = pl.BlockSpec(memory_space=pltpu.VMEM)
    dma = pltpu.SemaphoreType.DMA
    return pl.pallas_call(
        functools.partial(exchange_kernel, groups, nfeat),
        out_shape=(
            jax.ShapeDtypeStruct((rows, width), jnp.bfloat16),
            jax.ShapeDtypeStruct((fcols, width), jnp.float32),
            jax.ShapeDtypeStruct((fcols, width), jnp.float32),
            jax.ShapeDtypeStruct((1, width), jnp.float32),
        ),
        in_specs=[any_spec] * (MERGE // 2 + 1) + [vmem_spec] * 2,
        out_specs=(vmem_spec,) * 4,
        scratch_shapes=[
            pltpu.VMEM((outer, MERGE, fcols, rows), jnp.bfloat16),
            pltpu.VMEM((outer, MERGE, fcols, rows), jnp.bfloat16),
            pltpu.VMEM((2, MERGE, fcols, width), jnp.bfloat16),
            pltpu.VMEM((outer, rows, width), jnp.bfloat16),
            pltpu.VMEM((outer, rows, width), jnp.bfloat16),
            pltpu.VMEM((outer, rows, width), jnp.bfloat16),
            pltpu.VMEM((2, MERGE, fcols, width), jnp.float32),
            pltpu.VMEM((MERGE // 2, 2 * fcols + 16, width), jnp.bfloat16),
            pltpu.VMEM((MERGE // 2, 2 * fcols + 16, width), jnp.bfloat16),
            pltpu.VMEM((MERGE // 2, 2 * fcols + 16, width), jnp.bfloat16),
            pltpu.VMEM((MERGE // 2, 2 * fcols + 16, width), jnp.bfloat16),
            pltpu.VMEM((2 * fcols + 16, width), jnp.float32),
            pltpu.VMEM((groups, 2 * fcols + 16, width), jnp.float32),
            dma((2, outer, MERGE)),
            dma((2, MERGE // 2, outer + 2)),
            dma((2, outer, PARTS)),
            dma((2, outer, PARTS)),
            dma((2, MERGE // 2)),
            dma((2, MERGE // 2)),
            dma((2, groups)),
            dma((MERGE // 2, outer + 2)),
            dma((outer,)),
        ],
        compiler_params=pltpu.CompilerParams(
            collective_id=0, has_side_effects=True, vmem_limit_bytes=40 * 2**20),
        name="exchange",
    )(*moved, aggregated, bias.reshape(1, width), upstream)


def finish_kernel(*refs):
    for source, target in zip(refs[:4], refs[4:]):
        target[...] = source[...]


def finish(*parts):
    return pl.pallas_call(
        finish_kernel,
        out_shape=tuple(jax.ShapeDtypeStruct(p.shape, p.dtype) for p in parts),
        name="finish",
    )(*parts)


def body(
    features_t, tile_weights, tile_dst, tile_src, tile_count, w_self, w_neigh, bias, grad_hidden
):
    feats = features_t[0]
    ndst = grad_hidden.shape[0] * lax.axis_size("feat")
    moved = arrange(feats, w_self, w_neigh, grad_hidden.shape[0])
    aggregated = aggregate(feats, tile_weights[0], tile_dst[0], tile_src[0], tile_count, ndst)
    hidden, grad_self, grad_neigh, grad_bias = finish(
        *exchange(moved, aggregated, bias, grad_hidden))
    return (hidden, grad_self, grad_neigh, grad_bias[0])


def solution(mesh):
    return jax.shard_map(
        body,
        mesh=mesh,
        in_specs=(
            P("vgroup", "feat", None),
            P("vgroup", None, None, None),
            P("vgroup", None),
            P("vgroup", None),
            P("vgroup"),
            P("feat", None),
            P("feat", None),
            P(),
            P(("vgroup", "feat"), None),
        ),
        out_specs=(P(("vgroup", "feat"), None), P("feat", None), P("feat", None), P()),
        check_vma=False,
    )
```

```python
import functools

import jax
import jax.numpy as jnp
from jax import lax
from jax.experimental import pallas as pl
from jax.experimental.pallas import tpu as pltpu
from jax.sharding import PartitionSpec as P

STEP = 64
UNROLL = 32


def aggregate_kernel(dst_ref, src_ref, count_ref, x_ref, w_ref, out_ref, acc_a, acc_b):
    step = pl.program_id(0)
    tile = w_ref.shape[1]
    dtiles = out_ref.shape[1] // tile
    base = step * STEP
    fcols = x_ref.shape[0]

    @pl.when(step == 0)
    def _():
        acc_a[...] = jnp.zeros_like(acc_a)
        acc_b[...] = jnp.zeros_like(acc_b)

    def place(i):
        t = base + i
        return jnp.where(t < count_ref[0], dst_ref[t], dtiles)

    @pl.loop(0, STEP // UNROLL)
    def _(group):
        for k in range(0, UNROLL, 4):
            i = group * UNROLL + k
            cols = [
                x_ref[:, pl.ds(pl.multiple_of(src_ref[base + i + n] * tile, tile), tile)]
                for n in range(4)
            ]
            zero = jnp.zeros_like(cols[0])
            left = jnp.concatenate([
                jnp.concatenate([cols[n], zero] if n % 2 == 0 else [zero, cols[n]], axis=1)
                for n in range(4)], axis=0)
            right = jnp.concatenate([
                jnp.concatenate([w_ref[i], w_ref[i + 1]], axis=1),
                jnp.concatenate([w_ref[i + 2], w_ref[i + 3]], axis=1)], axis=0)
            prod = lax.dot_general(
                left, right, (((1,), (1,)), ((), ())), preferred_element_type=jnp.float32)
            for n in range(4):
                d = place(i + n)
                acc = (acc_a, acc_b)[n % 2]
                half = n // 2 * tile
                acc[d] = acc[d] + prod[n * fcols:(n + 1) * fcols, half:half + tile]

    @pl.when(step == pl.num_programs(0) - 1)
    def _():
        for d in range(dtiles):
            out_ref[:, d * tile:(d + 1) * tile] = (acc_a[d] + acc_b[d]).astype(out_ref.dtype)


def aggregate(feats, tiles, dsts, srcs, count, ndst):
    fcols, nsrc = feats.shape
    total, tile, _ = tiles.shape
    return pl.pallas_call(
        aggregate_kernel,
        grid_spec=pltpu.PrefetchScalarGridSpec(
            num_scalar_prefetch=3,
            grid=(total // STEP,),
            in_specs=[
                pl.BlockSpec((fcols, nsrc), lambda i, *_: (0, 0), pipeline_mode=pl.Buffered(1)),
                pl.BlockSpec((STEP, tile, tile), lambda i, *_: (i, 0, 0)),
            ],
            out_specs=pl.BlockSpec((fcols, ndst), lambda i, *_: (0, 0), pipeline_mode=pl.Buffered(1)),
            scratch_shapes=[pltpu.VMEM((ndst // tile + 1, fcols, tile), jnp.float32)] * 2,
        ),
        out_shape=jax.ShapeDtypeStruct((fcols, ndst), jnp.bfloat16),
        compiler_params=pltpu.CompilerParams(vmem_limit_bytes=60 * 2**20),
        cost_estimate=pl.CostEstimate(
            flops=2 * total * fcols * tile * tile, bytes_accessed=total * tile * tile * 2,
            transcendentals=0,
        ),
        name="aggregate",
    )(dsts, srcs, count, feats, tiles)


MERGE = 8
PARTS = 2
CUBIC = 0.044715
ROOT = 0.7978845608


def arrange_kernel(outer, x_ref, ws_ref, wn_ref, *refs):
    outs = refs
    fcols, width = ws_ref.shape
    rows = outs[0].shape[1]
    me = lax.axis_index("feat")
    for p, out in enumerate(outs):
        for side in range(2):
            for j in range(outer):
                owner = me ^ (j * MERGE + 2 * p + side)
                columns = pl.ds(pl.multiple_of(owner * rows, rows), rows)
                place = side * outer + j
                out[place * fcols:(place + 1) * fcols] = x_ref[:, columns]
        last = slice(2 * outer * fcols, (2 * outer + 1) * fcols)
        out[last, 0:width] = ws_ref[...]
        out[last, width:2 * width] = wn_ref[...]


def arrange(feats, w_self, w_neigh, rows):
    outer = lax.axis_size("feat") // MERGE
    fcols, width = w_self.shape
    nfeat = lax.axis_size("feat")
    pieces = pl.pallas_call(
        functools.partial(arrange_kernel, outer),
        out_shape=(jax.ShapeDtypeStruct(((2 * outer + 1) * fcols, rows), jnp.bfloat16),) * (MERGE // 2),
        grid=(1,),
        in_specs=[
            pl.BlockSpec((fcols, rows * nfeat), lambda i: (0, 0)),
            pl.BlockSpec((fcols, width), lambda i: (0, 0)),
            pl.BlockSpec((fcols, width), lambda i: (0, 0)),
        ],
        out_specs=(pl.BlockSpec(((2 * outer + 1) * fcols, rows), lambda i: (0, 0)),) * (MERGE // 2),
        compiler_params=pltpu.CompilerParams(vmem_limit_bytes=60 * 2**20),
        name="arrange",
    )(feats, w_self, w_neigh)
    moved = [pieces[0]]
    for p in range(1, MERGE // 2):
        moved.append(lax.ppermute(pieces[p], "feat", [(f, f ^ (2 * p)) for f in range(nfeat)]))
    return moved


def exchange_kernel(
    groups, nfeat,
    *refs,
):
    moved, refs = refs[:MERGE // 2], refs[MERGE // 2:]
    a_ref, bias_ref, up_ref, hidden_ref, gs_ref, gn_ref, gb_ref, *refs = refs
    xm, am, wm, psend, precv, dall, gacc, gsend, gpair, gout, grecv, vsend, vrecv, *refs = refs
    a_sems, s_sems, p_sems, d_sems, h_sems, g_sems, v_sems, l_sems, own_sems = refs
    outer = nfeat // MERGE
    fcols = a_ref.shape[0]
    rows = up_ref.shape[0]
    width = up_ref.shape[1]
    grp = lax.axis_index("vgroup")
    me = lax.axis_index("feat")
    lo = lax.rem(me, MERGE)
    hi = lax.div(me, MERGE)

    def inner_peer(k):
        return (grp, hi * MERGE + (lo ^ k))

    def outer_peer(j):
        return (grp, (hi ^ j) * MERGE + lo)

    def group_peer(j):
        return (grp ^ j, me)

    peers = [inner_peer(k) for k in range(1, MERGE)]
    peers += [outer_peer(j) for j in range(1, outer)]
    peers += [group_peer(j) for j in range(1, groups)]
    barrier = pltpu.get_barrier_semaphore()
    for peer in peers:
        pl.semaphore_signal(barrier, inc=1, device_id=peer, device_id_type=pl.DeviceIdType.MESH)
    pl.semaphore_wait(barrier, len(peers))

    def remote(source, target, sems, index, peer):
        copy = pltpu.make_async_remote_copy(
            src_ref=source, dst_ref=target,
            send_sem=sems.at[(0,) + index], recv_sem=sems.at[(1,) + index],
            device_id=peer, device_id_type=pl.DeviceIdType.MESH,
        )
        copy.start()
        return copy

    def columns(j, k):
        owner = (hi ^ j) * MERGE + (lo ^ k)
        return pl.ds(pl.multiple_of(owner * rows, rows), rows)

    order = list(range(1, outer)) + [0]
    pending = []
    local = []
    got = {}

    steps = [(j, c) for j in order for c in range(PARTS)]
    part_rows = rows // PARTS

    def send_columns(j, c):
        got[j, c] = []
        for k in range(1, MERGE):
            owner = (hi ^ j) * MERGE + (lo ^ k)
            source = pl.ds(pl.multiple_of(owner * rows + c * part_rows, part_rows), part_rows)
            got[j, c].append(remote(
                a_ref.at[:, source], am.at[j, k, :, pl.ds(c * part_rows, part_rows)],
                a_sems, (j, c, k), inner_peer(k)))

    send_columns(*steps[0])
    for j in order:
        local.append(pltpu.make_async_copy(a_ref.at[:, columns(j, 0)], am.at[j, 0], own_sems.at[j]))
    shared = []
    for p, piece in enumerate(moved):
        k = 2 * p
        for j in range(outer):
            local.append(pltpu.make_async_copy(
                piece.at[pl.ds(j * fcols, fcols)], xm.at[j, k], l_sems.at[p, j]))
            shared.append(remote(
                piece.at[pl.ds((outer + j) * fcols, fcols)], xm.at[j, k + 1],
                s_sems, (p, j), inner_peer(1)))
        for i in range(2):
            weights = piece.at[pl.ds(2 * outer * fcols, fcols), pl.ds(i * width, width)]
            local.append(pltpu.make_async_copy(weights, wm.at[i, k], l_sems.at[p, outer + i]))
            shared.append(remote(weights, wm.at[i, k + 1], s_sems, (p, outer + i), inner_peer(1)))
    for copy in local:
        copy.start()
    for copy in local:
        copy.wait()
    for copy in shared:
        copy.wait_recv()
    pending += shared

    merged_cols = MERGE * fcols

    def partial_pre(j, c):
        span = slice(c * part_rows, (c + 1) * part_rows)
        total = lax.dot_general(
            xm[j, :, :, span].reshape(merged_cols, part_rows), wm[0].reshape(merged_cols, width),
            (((0,), (0,)), ((), ())), preferred_element_type=jnp.float32)
        for copy in got[j, c]:
            copy.wait_recv()
        pending.extend(got[j, c])
        if j > 0:
            later = steps.index((j, c)) + 1
            for step in steps[later:later + 1] if steps[later][0] > 0 else steps[later:]:
                send_columns(*step)
        return total + lax.dot_general(
            am[j, :, :, span].reshape(merged_cols, part_rows), wm[1].reshape(merged_cols, width),
            (((0,), (0,)), ((), ())), preferred_element_type=jnp.float32)

    def grads(j, c, colsum):
        span = slice(c * part_rows, (c + 1) * part_rows)
        delta = dall[j, span]
        for i, merged in enumerate((xm, am)):
            part = jnp.dot(
                merged[j, :, :, span].reshape(merged_cols, part_rows), delta,
                preferred_element_type=jnp.float32,
            ).reshape(MERGE, fcols, width)
            if j == 0 and c == 0:
                gacc[i] = part
            else:
                gacc[i] = gacc[i] + part
        return colsum + jnp.sum(delta.astype(jnp.float32), axis=0, keepdims=True)

    sent = {}
    for j in range(1, outer):
        for c in range(PARTS):
            span = pl.ds(c * part_rows, part_rows)
            psend[j, span] = partial_pre(j, c).astype(psend.dtype)
            sent[j, c] = remote(
                psend.at[j, span], precv.at[j, span], p_sems, (j, c), outer_peer(j))
    deltas = {}
    for c in range(PARTS):
        span = pl.ds(c * part_rows, part_rows)
        pre = partial_pre(0, c) + bias_ref[...]
        for j in range(1, outer):
            sent[j, c].wait_recv()
            pre = pre + precv[j, span].astype(jnp.float32)
        square = pre * pre
        t = jnp.tanh(ROOT * pre * (1.0 + CUBIC * square))
        half = 0.5 * (1.0 + t)
        slope = half + 0.5 * pre * (1.0 - t * t) * (ROOT * (1.0 + 3.0 * CUBIC * square))
        dall[0, span] = (slope * up_ref[span].astype(jnp.float32)).astype(dall.dtype)
        for j in range(1, outer):
            deltas[j, c] = remote(
                dall.at[0, span], dall.at[j, span], d_sems, (j, c), outer_peer(j))
        hidden_ref[span] = (pre * half).astype(hidden_ref.dtype)
    pending += list(sent.values())
    pending += list(deltas.values())

    colsum = jnp.zeros((1, width), jnp.float32)
    for c in range(PARTS):
        colsum = grads(0, c, colsum)
    for c in range(PARTS):
        for j in range(1, outer):
            deltas[j, c].wait_recv()
            colsum = grads(j, c, colsum)
    row_id = lax.broadcasted_iota(jnp.int32, (16, width), 0)
    tail = slice(2 * fcols, 2 * fcols + 16)

    def split(value):
        high = value.astype(jnp.bfloat16).astype(jnp.float32)
        return jnp.where(
            row_id == 0, high, jnp.where(row_id == 1, value - high, 0.0)).astype(jnp.bfloat16)

    def join(block):
        return jnp.sum(block.astype(jnp.float32), axis=0, keepdims=True)

    tag = split(colsum)
    pairs = MERGE // 2
    sent = {}
    for m in list(range(1, pairs)) + [0]:
        gsend[m, 0:fcols] = gacc[0, 2 * m + 1].astype(gsend.dtype)
        gsend[m, fcols:2 * fcols] = gacc[1, 2 * m + 1].astype(gsend.dtype)
        gsend[m, tail] = tag
        sent[m] = remote(gsend.at[m], gpair.at[m], h_sems, (m,), inner_peer(1))
    passed = {}
    for m in range(1, pairs):
        sent[m].wait_recv()
        if m == 1:
            colsum = colsum + join(gpair[1, tail])
            tag = split(colsum)
        gout[m, 0:fcols] = (gacc[0, 2 * m] + gpair[m, 0:fcols].astype(jnp.float32)).astype(gout.dtype)
        gout[m, fcols:2 * fcols] = (
            gacc[1, 2 * m] + gpair[m, fcols:2 * fcols].astype(jnp.float32)).astype(gout.dtype)
        gout[m, tail] = tag
        passed[m] = remote(gout.at[m], grecv.at[m], g_sems, (m,), inner_peer(2 * m))
    sent[0].wait_recv()
    total_s = gacc[0, 0] + gpair[0, 0:fcols].astype(jnp.float32)
    total_n = gacc[1, 0] + gpair[0, fcols:2 * fcols].astype(jnp.float32)
    for m in range(1, pairs):
        passed[m].wait_recv()
        total_s = total_s + grecv[m, 0:fcols].astype(jnp.float32)
        total_n = total_n + grecv[m, fcols:2 * fcols].astype(jnp.float32)
        colsum = colsum + join(grecv[m, tail])
    pending += list(sent.values())
    pending += list(passed.values())
    vsend[0:fcols] = total_s.astype(vsend.dtype)
    vsend[fcols:2 * fcols] = total_n.astype(vsend.dtype)
    vsend[tail] = split(colsum)
    sent = [remote(vsend, vrecv.at[j], v_sems, (j,), group_peer(j)) for j in range(1, groups)]
    for j in range(1, groups):
        sent[j - 1].wait_recv()
        total_s = total_s + vrecv[j, 0:fcols].astype(jnp.float32)
        total_n = total_n + vrecv[j, fcols:2 * fcols].astype(jnp.float32)
        colsum = colsum + join(vrecv[j, tail])
    pending += sent
    gs_ref[...] = total_s
    gn_ref[...] = total_n
    gb_ref[...] = colsum
    for copy in pending:
        copy.wait_send()


def exchange(moved, aggregated, bias, upstream):
    groups = lax.axis_size("vgroup")
    nfeat = lax.axis_size("feat")
    outer = nfeat // MERGE
    fcols = aggregated.shape[0]
    rows, width = upstream.shape
    any_spec = pl.BlockSpec(memory_space=pl.ANY)
    vmem_spec = pl.BlockSpec(memory_space=pltpu.VMEM)
    dma = pltpu.SemaphoreType.DMA
    return pl.pallas_call(
        functools.partial(exchange_kernel, groups, nfeat),
        out_shape=(
            jax.ShapeDtypeStruct((rows, width), jnp.bfloat16),
            jax.ShapeDtypeStruct((fcols, width), jnp.float32),
            jax.ShapeDtypeStruct((fcols, width), jnp.float32),
            jax.ShapeDtypeStruct((1, width), jnp.float32),
        ),
        in_specs=[any_spec] * (MERGE // 2 + 1) + [vmem_spec] * 2,
        out_specs=(vmem_spec,) * 4,
        scratch_shapes=[
            pltpu.VMEM((outer, MERGE, fcols, rows), jnp.bfloat16),
            pltpu.VMEM((outer, MERGE, fcols, rows), jnp.bfloat16),
            pltpu.VMEM((2, MERGE, fcols, width), jnp.bfloat16),
            pltpu.VMEM((outer, rows, width), jnp.bfloat16),
            pltpu.VMEM((outer, rows, width), jnp.bfloat16),
            pltpu.VMEM((outer, rows, width), jnp.bfloat16),
            pltpu.VMEM((2, MERGE, fcols, width), jnp.float32),
            pltpu.VMEM((MERGE // 2, 2 * fcols + 16, width), jnp.bfloat16),
            pltpu.VMEM((MERGE // 2, 2 * fcols + 16, width), jnp.bfloat16),
            pltpu.VMEM((MERGE // 2, 2 * fcols + 16, width), jnp.bfloat16),
            pltpu.VMEM((MERGE // 2, 2 * fcols + 16, width), jnp.bfloat16),
            pltpu.VMEM((2 * fcols + 16, width), jnp.bfloat16),
            pltpu.VMEM((groups, 2 * fcols + 16, width), jnp.bfloat16),
            dma((2, outer, PARTS, MERGE)),
            dma((2, MERGE // 2, outer + 2)),
            dma((2, outer, PARTS)),
            dma((2, outer, PARTS)),
            dma((2, MERGE // 2)),
            dma((2, MERGE // 2)),
            dma((2, groups)),
            dma((MERGE // 2, outer + 2)),
            dma((outer,)),
        ],
        compiler_params=pltpu.CompilerParams(
            collective_id=0, has_side_effects=True, vmem_limit_bytes=62 * 2**20),
        name="exchange",
    )(*moved, aggregated, bias.reshape(1, width), upstream)


def body(
    features_t, tile_weights, tile_dst, tile_src, tile_count, w_self, w_neigh, bias, grad_hidden
):
    feats = features_t[0]
    ndst = grad_hidden.shape[0] * lax.axis_size("feat")
    moved = arrange(feats, w_self, w_neigh, grad_hidden.shape[0])
    aggregated = aggregate(feats, tile_weights[0], tile_dst[0], tile_src[0], tile_count, ndst)
    hidden, grad_self, grad_neigh, grad_bias = exchange(moved, aggregated, bias, grad_hidden)
    return (hidden, grad_self, grad_neigh, grad_bias[0])


def solution(mesh):
    return jax.shard_map(
        body,
        mesh=mesh,
        in_specs=(
            P("vgroup", "feat", None),
            P("vgroup", None, None, None),
            P("vgroup", None),
            P("vgroup", None),
            P("vgroup"),
            P("feat", None),
            P("feat", None),
            P(),
            P(("vgroup", "feat"), None),
        ),
        out_specs=(P(("vgroup", "feat"), None), P("feat", None), P("feat", None), P()),
        check_vma=False,
    )
```

```python
import functools

import jax
import jax.numpy as jnp
from jax import lax
from jax.experimental import pallas as pl
from jax.experimental.pallas import tpu as pltpu
from jax.sharding import PartitionSpec as P

STEP = 32
PACK = 16


def aggregate_kernel(
    dst_ref, src_ref, count_ref, x_any, w_any, out_ref, x_ref, w_ref, acc_a, acc_b, x_sems, w_sems
):
    fcols = x_any.shape[0]
    total, tile, _ = w_any.shape
    dtiles = out_ref.shape[1] // tile

    x_copies = [
        pltpu.make_async_copy(
            x_any.at[pl.ds(q * PACK, PACK)], x_ref.at[pl.ds(q * PACK, PACK)], x_sems.at[q])
        for q in range(fcols // PACK)
    ]

    def w_copy(step):
        span = pl.ds(step * STEP, STEP)
        return pltpu.make_async_copy(w_any.at[span], w_ref.at[span], w_sems.at[step])

    for copy in x_copies:
        copy.start()
    for step in range(total // STEP):
        w_copy(step).start()
    acc_a[...] = jnp.zeros_like(acc_a)
    acc_b[...] = jnp.zeros_like(acc_b)
    for copy in x_copies:
        copy.wait()

    def place(t):
        return jnp.where(t < count_ref[0], dst_ref[t], dtiles)

    @pl.loop(0, total // STEP)
    def _(step):
        w_copy(step).wait()
        for k in range(0, STEP, 2):
            t = step * STEP + k
            one, two = [
                x_ref[:, pl.ds(pl.multiple_of(src_ref[t + n] * tile, tile), tile)]
                for n in range(2)
            ]
            zero = jnp.zeros_like(one)
            left = jnp.concatenate([
                jnp.concatenate([one, zero], axis=1), jnp.concatenate([zero, two], axis=1)], axis=0)
            right = jnp.concatenate([w_ref[t], w_ref[t + 1]], axis=1)
            prod = lax.dot_general(
                left, right, (((1,), (1,)), ((), ())), preferred_element_type=jnp.float32)
            a, b = place(t), place(t + 1)
            acc_a[a] = acc_a[a] + prod[:fcols]
            acc_b[b] = acc_b[b] + prod[fcols:]

    for d in range(dtiles):
        out_ref[:, d * tile:(d + 1) * tile] = (acc_a[d] + acc_b[d]).astype(out_ref.dtype)


def aggregate(feats, tiles, dsts, srcs, count, ndst):
    fcols, nsrc = feats.shape
    total, tile, _ = tiles.shape
    smem = pl.BlockSpec(memory_space=pltpu.SMEM)
    any_spec = pl.BlockSpec(memory_space=pl.ANY)
    return pl.pallas_call(
        aggregate_kernel,
        in_specs=[smem, smem, smem, any_spec, any_spec],
        out_specs=pl.BlockSpec(memory_space=pltpu.VMEM),
        scratch_shapes=[
            pltpu.VMEM((fcols, nsrc), jnp.bfloat16),
            pltpu.VMEM((total, tile, tile), jnp.bfloat16),
            pltpu.VMEM((ndst // tile + 1, fcols, tile), jnp.float32),
            pltpu.VMEM((ndst // tile + 1, fcols, tile), jnp.float32),
            pltpu.SemaphoreType.DMA((fcols // PACK,)),
            pltpu.SemaphoreType.DMA((total // STEP,)),
        ],
        out_shape=jax.ShapeDtypeStruct((fcols, ndst), jnp.bfloat16),
        compiler_params=pltpu.CompilerParams(vmem_limit_bytes=60 * 2**20),
        cost_estimate=pl.CostEstimate(
            flops=2 * total * fcols * tile * tile, bytes_accessed=total * tile * tile * 2,
            transcendentals=0,
        ),
        name="aggregate",
    )(dsts, srcs, count, feats, tiles)


MERGE = 8
PARTS = 2
CUBIC = 0.044715
ROOT = 0.7978845608


def arrange_kernel(outer, ws_ref, wn_ref, *refs):
    fcols, width = ws_ref.shape
    bands = fcols // PACK
    x_refs, outs = refs[:bands], refs[bands:]
    rows = outs[0].shape[1]
    me = lax.axis_index("feat")
    for p, out in enumerate(outs):
        for side in range(2):
            for j in range(outer):
                owner = me ^ (j * MERGE + 2 * p + side)
                columns = pl.ds(pl.multiple_of(owner * rows, rows), rows)
                for q in range(bands):
                    first = (side * outer + j) * fcols + q * PACK
                    out[first:first + PACK] = x_refs[q][:, columns]
        last = slice(2 * outer * fcols, (2 * outer + 1) * fcols)
        out[last, 0:width] = ws_ref[...]
        out[last, width:2 * width] = wn_ref[...]


def arrange(feats, w_self, w_neigh, rows):
    nfeat = lax.axis_size("feat")
    outer = nfeat // MERGE
    fcols, width = w_self.shape
    bands = fcols // PACK
    whole = pl.BlockSpec((fcols, width), lambda i: (0, 0))
    pieces = pl.pallas_call(
        functools.partial(arrange_kernel, outer),
        out_shape=(
            jax.ShapeDtypeStruct(((2 * outer + 1) * fcols, rows), jnp.bfloat16),) * (MERGE // 2),
        grid=(1,),
        in_specs=[whole, whole] + [
            pl.BlockSpec((PACK, rows * nfeat), lambda i, q=q: (q, 0)) for q in range(bands)],
        out_specs=(pl.BlockSpec(((2 * outer + 1) * fcols, rows), lambda i: (0, 0)),) * (MERGE // 2),
        compiler_params=pltpu.CompilerParams(vmem_limit_bytes=60 * 2**20),
        name="arrange",
    )(w_self, w_neigh, *[feats] * bands)
    moved = [pieces[0]]
    for p in range(1, MERGE // 2):
        moved.append(lax.ppermute(pieces[p], "feat", [(f, f ^ (2 * p)) for f in range(nfeat)]))
    return moved


def exchange_kernel(
    groups, nfeat,
    *refs,
):
    moved, refs = refs[:MERGE // 2], refs[MERGE // 2:]
    a_ref, bias_ref, up_ref, hidden_ref, gs_ref, gn_ref, gb_ref, *refs = refs
    xm, am, wm, psend, precv, dall, gacc, gsend, gpair, gout, grecv, vsend, vrecv, *refs = refs
    a_sems, s_sems, p_sems, d_sems, h_sems, g_sems, v_sems, l_sems, own_sems = refs
    outer = nfeat // MERGE
    fcols = a_ref.shape[0]
    rows = up_ref.shape[0]
    width = up_ref.shape[1]
    grp = lax.axis_index("vgroup")
    me = lax.axis_index("feat")
    lo = lax.rem(me, MERGE)
    hi = lax.div(me, MERGE)

    def inner_peer(k):
        return (grp, hi * MERGE + (lo ^ k))

    def outer_peer(j):
        return (grp, (hi ^ j) * MERGE + lo)

    def group_peer(j):
        return (grp ^ j, me)

    peers = [inner_peer(k) for k in range(1, MERGE)]
    peers += [outer_peer(j) for j in range(1, outer)]
    peers += [group_peer(j) for j in range(1, groups)]
    barrier = pltpu.get_barrier_semaphore()
    for peer in peers:
        pl.semaphore_signal(barrier, inc=1, device_id=peer, device_id_type=pl.DeviceIdType.MESH)
    pl.semaphore_wait(barrier, len(peers))

    def remote(source, target, sems, index, peer):
        copy = pltpu.make_async_remote_copy(
            src_ref=source, dst_ref=target,
            send_sem=sems.at[(0,) + index], recv_sem=sems.at[(1,) + index],
            device_id=peer, device_id_type=pl.DeviceIdType.MESH,
        )
        copy.start()
        return copy

    def columns(j, k):
        owner = (hi ^ j) * MERGE + (lo ^ k)
        return pl.ds(pl.multiple_of(owner * rows, rows), rows)

    order = list(range(1, outer)) + [0]
    pending = []
    local = []
    got = {}

    def send_columns(j):
        got[j] = [
            remote(a_ref.at[:, columns(j, k)], am.at[j, k], a_sems, (j, k), inner_peer(k))
            for k in range(1, MERGE)
        ]

    send_columns(order[0])
    for j in order:
        local.append(pltpu.make_async_copy(a_ref.at[:, columns(j, 0)], am.at[j, 0], own_sems.at[j]))
    shared = []
    for p, piece in enumerate(moved):
        k = 2 * p
        for j in range(outer):
            local.append(pltpu.make_async_copy(
                piece.at[pl.ds(j * fcols, fcols)], xm.at[j, k], l_sems.at[p, j]))
            shared.append(remote(
                piece.at[pl.ds((outer + j) * fcols, fcols)], xm.at[j, k + 1],
                s_sems, (p, j), inner_peer(1)))
        for i in range(2):
            weights = piece.at[pl.ds(2 * outer * fcols, fcols), pl.ds(i * width, width)]
            local.append(pltpu.make_async_copy(weights, wm.at[i, k], l_sems.at[p, outer + i]))
            shared.append(remote(weights, wm.at[i, k + 1], s_sems, (p, outer + i), inner_peer(1)))
    for copy in local:
        copy.start()
    for copy in local:
        copy.wait()
    for copy in shared:
        copy.wait_recv()
    pending += shared

    merged_cols = MERGE * fcols

    part_rows = rows // PARTS

    def partial_pre(j, c):
        span = slice(c * part_rows, (c + 1) * part_rows)
        total = lax.dot_general(
            xm[j, :, :, span].reshape(merged_cols, part_rows), wm[0].reshape(merged_cols, width),
            (((0,), (0,)), ((), ())), preferred_element_type=jnp.float32)
        if c == 0:
            for copy in got[j]:
                copy.wait_recv()
            pending.extend(got[j])
            if j > 0:
                send_columns(order[order.index(j) + 1])
        return total + lax.dot_general(
            am[j, :, :, span].reshape(merged_cols, part_rows), wm[1].reshape(merged_cols, width),
            (((0,), (0,)), ((), ())), preferred_element_type=jnp.float32)

    def grads(j, c, colsum):
        span = slice(c * part_rows, (c + 1) * part_rows)
        delta = dall[j, span]
        for i, merged in enumerate((xm, am)):
            part = jnp.dot(
                merged[j, :, :, span].reshape(merged_cols, part_rows), delta,
                preferred_element_type=jnp.float32,
            ).reshape(MERGE, fcols, width)
            if j == 0 and c == 0:
                gacc[i] = part
            else:
                gacc[i] = gacc[i] + part
        return colsum + jnp.sum(delta.astype(jnp.float32), axis=0, keepdims=True)

    sent = {}
    for j in range(1, outer):
        for c in range(PARTS):
            span = pl.ds(c * part_rows, part_rows)
            psend[j, span] = partial_pre(j, c).astype(psend.dtype)
            sent[j, c] = remote(
                psend.at[j, span], precv.at[j, span], p_sems, (j, c), outer_peer(j))
    deltas = {}
    for c in range(PARTS):
        span = pl.ds(c * part_rows, part_rows)
        pre = partial_pre(0, c) + bias_ref[...]
        for j in range(1, outer):
            sent[j, c].wait_recv()
            pre = pre + precv[j, span].astype(jnp.float32)
        square = pre * pre
        t = jnp.tanh(ROOT * pre * (1.0 + CUBIC * square))
        half = 0.5 * (1.0 + t)
        slope = half + 0.5 * pre * (1.0 - t * t) * (ROOT * (1.0 + 3.0 * CUBIC * square))
        dall[0, span] = (slope * up_ref[span].astype(jnp.float32)).astype(dall.dtype)
        for j in range(1, outer):
            deltas[j, c] = remote(
                dall.at[0, span], dall.at[j, span], d_sems, (j, c), outer_peer(j))
        hidden_ref[span] = (pre * half).astype(hidden_ref.dtype)
    pending += list(sent.values())
    pending += list(deltas.values())

    colsum = jnp.zeros((1, width), jnp.float32)
    for c in range(PARTS):
        colsum = grads(0, c, colsum)
    for c in range(PARTS):
        for j in range(1, outer):
            deltas[j, c].wait_recv()
            colsum = grads(j, c, colsum)
    row_id = lax.broadcasted_iota(jnp.int32, (16, width), 0)
    tail = slice(2 * fcols, 2 * fcols + 16)

    def split(value):
        high = value.astype(jnp.bfloat16).astype(jnp.float32)
        return jnp.where(
            row_id == 0, high, jnp.where(row_id == 1, value - high, 0.0)).astype(jnp.bfloat16)

    def join(block):
        return jnp.sum(block.astype(jnp.float32), axis=0, keepdims=True)

    tag = split(colsum)
    pairs = MERGE // 2
    sent = {}
    for m in list(range(1, pairs)) + [0]:
        gsend[m, 0:fcols] = gacc[0, 2 * m + 1].astype(gsend.dtype)
        gsend[m, fcols:2 * fcols] = gacc[1, 2 * m + 1].astype(gsend.dtype)
        gsend[m, tail] = tag
        sent[m] = remote(gsend.at[m], gpair.at[m], h_sems, (m,), inner_peer(1))
    passed = {}
    for m in range(1, pairs):
        sent[m].wait_recv()
        if m == 1:
            colsum = colsum + join(gpair[1, tail])
            tag = split(colsum)
        gout[m, 0:fcols] = (gacc[0, 2 * m] + gpair[m, 0:fcols].astype(jnp.float32)).astype(gout.dtype)
        gout[m, fcols:2 * fcols] = (
            gacc[1, 2 * m] + gpair[m, fcols:2 * fcols].astype(jnp.float32)).astype(gout.dtype)
        gout[m, tail] = tag
        passed[m] = remote(gout.at[m], grecv.at[m], g_sems, (m,), inner_peer(2 * m))
    sent[0].wait_recv()
    total_s = gacc[0, 0] + gpair[0, 0:fcols].astype(jnp.float32)
    total_n = gacc[1, 0] + gpair[0, fcols:2 * fcols].astype(jnp.float32)
    for m in range(1, pairs):
        passed[m].wait_recv()
        total_s = total_s + grecv[m, 0:fcols].astype(jnp.float32)
        total_n = total_n + grecv[m, fcols:2 * fcols].astype(jnp.float32)
        colsum = colsum + join(grecv[m, tail])
    pending += list(sent.values())
    pending += list(passed.values())
    vsend[0:fcols] = total_s.astype(vsend.dtype)
    vsend[fcols:2 * fcols] = total_n.astype(vsend.dtype)
    vsend[tail] = split(colsum)
    sent = [remote(vsend, vrecv.at[j], v_sems, (j,), group_peer(j)) for j in range(1, groups)]
    for j in range(1, groups):
        sent[j - 1].wait_recv()
        total_s = total_s + vrecv[j, 0:fcols].astype(jnp.float32)
        total_n = total_n + vrecv[j, fcols:2 * fcols].astype(jnp.float32)
        colsum = colsum + join(vrecv[j, tail])
    pending += sent
    gs_ref[...] = total_s
    gn_ref[...] = total_n
    gb_ref[...] = colsum
    for copy in pending:
        copy.wait_send()


def exchange(moved, aggregated, bias, upstream):
    groups = lax.axis_size("vgroup")
    nfeat = lax.axis_size("feat")
    outer = nfeat // MERGE
    fcols = aggregated.shape[0]
    rows, width = upstream.shape
    any_spec = pl.BlockSpec(memory_space=pl.ANY)
    vmem_spec = pl.BlockSpec(memory_space=pltpu.VMEM)
    dma = pltpu.SemaphoreType.DMA
    return pl.pallas_call(
        functools.partial(exchange_kernel, groups, nfeat),
        out_shape=(
            jax.ShapeDtypeStruct((rows, width), jnp.bfloat16),
            jax.ShapeDtypeStruct((fcols, width), jnp.float32),
            jax.ShapeDtypeStruct((fcols, width), jnp.float32),
            jax.ShapeDtypeStruct((1, width), jnp.float32),
        ),
        in_specs=[any_spec] * (MERGE // 2 + 1) + [vmem_spec] * 2,
        out_specs=(vmem_spec,) * 4,
        scratch_shapes=[
            pltpu.VMEM((outer, MERGE, fcols, rows), jnp.bfloat16),
            pltpu.VMEM((outer, MERGE, fcols, rows), jnp.bfloat16),
            pltpu.VMEM((2, MERGE, fcols, width), jnp.bfloat16),
            pltpu.VMEM((outer, rows, width), jnp.bfloat16),
            pltpu.VMEM((outer, rows, width), jnp.bfloat16),
            pltpu.VMEM((outer, rows, width), jnp.bfloat16),
            pltpu.VMEM((2, MERGE, fcols, width), jnp.float32),
            pltpu.VMEM((MERGE // 2, 2 * fcols + 16, width), jnp.bfloat16),
            pltpu.VMEM((MERGE // 2, 2 * fcols + 16, width), jnp.bfloat16),
            pltpu.VMEM((MERGE // 2, 2 * fcols + 16, width), jnp.bfloat16),
            pltpu.VMEM((MERGE // 2, 2 * fcols + 16, width), jnp.bfloat16),
            pltpu.VMEM((2 * fcols + 16, width), jnp.bfloat16),
            pltpu.VMEM((groups, 2 * fcols + 16, width), jnp.bfloat16),
            dma((2, outer, MERGE)),
            dma((2, MERGE // 2, outer + 2)),
            dma((2, outer, PARTS)),
            dma((2, outer, PARTS)),
            dma((2, MERGE // 2)),
            dma((2, MERGE // 2)),
            dma((2, groups)),
            dma((MERGE // 2, outer + 2)),
            dma((outer,)),
        ],
        compiler_params=pltpu.CompilerParams(
            collective_id=0, has_side_effects=True, vmem_limit_bytes=40 * 2**20),
        name="exchange",
    )(*moved, aggregated, bias.reshape(1, width), upstream)


def body(
    features_t, tile_weights, tile_dst, tile_src, tile_count, w_self, w_neigh, bias, grad_hidden
):
    feats = features_t[0]
    ndst = grad_hidden.shape[0] * lax.axis_size("feat")
    moved = arrange(feats, w_self, w_neigh, grad_hidden.shape[0])
    aggregated = aggregate(feats, tile_weights[0], tile_dst[0], tile_src[0], tile_count, ndst)
    hidden, grad_self, grad_neigh, grad_bias = exchange(moved, aggregated, bias, grad_hidden)
    return (hidden, grad_self, grad_neigh, grad_bias[0])


def solution(mesh):
    return jax.shard_map(
        body,
        mesh=mesh,
        in_specs=(
            P("vgroup", "feat", None),
            P("vgroup", None, None, None),
            P("vgroup", None),
            P("vgroup", None),
            P("vgroup"),
            P("feat", None),
            P("feat", None),
            P(),
            P(("vgroup", "feat"), None),
        ),
        out_specs=(P(("vgroup", "feat"), None), P("feat", None), P("feat", None), P()),
        check_vma=False,
    )
```

```python
import functools

import jax
import jax.numpy as jnp
from jax import lax
from jax.experimental import pallas as pl
from jax.experimental.pallas import tpu as pltpu
from jax.sharding import PartitionSpec as P

STREAMS = 4
BATCH = 16
STEP = STREAMS * BATCH
PACK = 16


def aggregate_kernel(dst_ref, src_ref, count_ref, x_ref, *refs):
    w_refs = refs[:STREAMS]
    out_ref, acc_a, acc_b = refs[STREAMS:]
    step = pl.program_id(0)
    fcols = x_ref.shape[0]
    tile = w_refs[0].shape[1]
    dtiles = out_ref.shape[1] // tile

    @pl.when(step == 0)
    def _():
        acc_a[...] = jnp.zeros_like(acc_a)
        acc_b[...] = jnp.zeros_like(acc_b)

    def place(t):
        return jnp.where(t < count_ref[0], dst_ref[t], dtiles)

    for q, w_ref in enumerate(w_refs):
        for k in range(0, BATCH, 2):
            t = step * STEP + q * BATCH + k
            one, two = [
                x_ref[:, pl.ds(pl.multiple_of(src_ref[t + n] * tile, tile), tile)]
                for n in range(2)
            ]
            zero = jnp.zeros_like(one)
            left = jnp.concatenate([
                jnp.concatenate([one, zero], axis=1), jnp.concatenate([zero, two], axis=1)], axis=0)
            right = jnp.concatenate([w_ref[k], w_ref[k + 1]], axis=1)
            prod = lax.dot_general(
                left, right, (((1,), (1,)), ((), ())), preferred_element_type=jnp.float32)
            a, b = place(t), place(t + 1)
            acc_a[a] = acc_a[a] + prod[:fcols]
            acc_b[b] = acc_b[b] + prod[fcols:]

    @pl.when(step == pl.num_programs(0) - 1)
    def _():
        for d in range(dtiles):
            out_ref[:, d * tile:(d + 1) * tile] = (acc_a[d] + acc_b[d]).astype(out_ref.dtype)


def aggregate(feats, tiles, dsts, srcs, count, ndst):
    fcols, nsrc = feats.shape
    total, tile, _ = tiles.shape
    return pl.pallas_call(
        aggregate_kernel,
        grid_spec=pltpu.PrefetchScalarGridSpec(
            num_scalar_prefetch=3,
            grid=(total // STEP,),
            in_specs=[
                pl.BlockSpec((fcols, nsrc), lambda i, *_: (0, 0), pipeline_mode=pl.Buffered(1)),
            ] + [
                pl.BlockSpec((BATCH, tile, tile), lambda i, *_, q=q: (i * STREAMS + q, 0, 0))
                for q in range(STREAMS)
            ],
            out_specs=pl.BlockSpec((fcols, ndst), lambda i, *_: (0, 0), pipeline_mode=pl.Buffered(1)),
            scratch_shapes=[pltpu.VMEM((ndst // tile + 1, fcols, tile), jnp.float32)] * 2,
        ),
        out_shape=jax.ShapeDtypeStruct((fcols, ndst), jnp.bfloat16),
        compiler_params=pltpu.CompilerParams(vmem_limit_bytes=60 * 2**20),
        cost_estimate=pl.CostEstimate(
            flops=2 * total * fcols * tile * tile, bytes_accessed=total * tile * tile * 2,
            transcendentals=0,
        ),
        name="aggregate",
    )(dsts, srcs, count, feats, *[tiles] * STREAMS)


MERGE = 8
PARTS = 2
CUBIC = 0.044715
ROOT = 0.7978845608


def arrange_kernel(outer, ws_ref, wn_ref, *refs):
    fcols, width = ws_ref.shape
    bands = fcols // PACK
    x_refs, outs = refs[:bands], refs[bands:]
    rows = outs[0].shape[1]
    me = lax.axis_index("feat")
    for p, out in enumerate(outs):
        for side in range(2):
            for j in range(outer):
                owner = me ^ (j * MERGE + 2 * p + side)
                columns = pl.ds(pl.multiple_of(owner * rows, rows), rows)
                for q in range(bands):
                    first = (side * outer + j) * fcols + q * PACK
                    out[first:first + PACK] = x_refs[q][:, columns]
        last = slice(2 * outer * fcols, (2 * outer + 1) * fcols)
        out[last, 0:width] = ws_ref[...]
        out[last, width:2 * width] = wn_ref[...]


def arrange(feats, w_self, w_neigh, rows):
    nfeat = lax.axis_size("feat")
    outer = nfeat // MERGE
    fcols, width = w_self.shape
    bands = fcols // PACK
    whole = pl.BlockSpec((fcols, width), lambda i: (0, 0))
    pieces = pl.pallas_call(
        functools.partial(arrange_kernel, outer),
        out_shape=(
            jax.ShapeDtypeStruct(((2 * outer + 1) * fcols, rows), jnp.bfloat16),) * (MERGE // 2),
        grid=(1,),
        in_specs=[whole, whole] + [
            pl.BlockSpec((PACK, rows * nfeat), lambda i, q=q: (q, 0)) for q in range(bands)],
        out_specs=(pl.BlockSpec(((2 * outer + 1) * fcols, rows), lambda i: (0, 0)),) * (MERGE // 2),
        compiler_params=pltpu.CompilerParams(vmem_limit_bytes=60 * 2**20),
        name="arrange",
    )(w_self, w_neigh, *[feats] * bands)
    moved = [pieces[0]]
    for p in range(1, MERGE // 2):
        moved.append(lax.ppermute(pieces[p], "feat", [(f, f ^ (2 * p)) for f in range(nfeat)]))
    return moved


def exchange_kernel(
    groups, nfeat,
    *refs,
):
    moved, refs = refs[:MERGE // 2], refs[MERGE // 2:]
    a_ref, bias_ref, up_ref, hidden_ref, gs_ref, gn_ref, gb_ref, *refs = refs
    xm, am, wm, psend, precv, dall, gacc, gsend, gpair, gout, grecv, vsend, vrecv, *refs = refs
    a_sems, s_sems, p_sems, d_sems, h_sems, g_sems, v_sems, l_sems, own_sems = refs
    outer = nfeat // MERGE
    fcols = a_ref.shape[0]
    rows = up_ref.shape[0]
    width = up_ref.shape[1]
    grp = lax.axis_index("vgroup")
    me = lax.axis_index("feat")
    lo = lax.rem(me, MERGE)
    hi = lax.div(me, MERGE)

    def inner_peer(k):
        return (grp, hi * MERGE + (lo ^ k))

    def outer_peer(j):
        return (grp, (hi ^ j) * MERGE + lo)

    def group_peer(j):
        return (grp ^ j, me)

    peers = [inner_peer(k) for k in range(1, MERGE)]
    peers += [outer_peer(j) for j in range(1, outer)]
    peers += [group_peer(j) for j in range(1, groups)]
    barrier = pltpu.get_barrier_semaphore()
    for peer in peers:
        pl.semaphore_signal(barrier, inc=1, device_id=peer, device_id_type=pl.DeviceIdType.MESH)
    pl.semaphore_wait(barrier, len(peers))

    def remote(source, target, sems, index, peer):
        copy = pltpu.make_async_remote_copy(
            src_ref=source, dst_ref=target,
            send_sem=sems.at[(0,) + index], recv_sem=sems.at[(1,) + index],
            device_id=peer, device_id_type=pl.DeviceIdType.MESH,
        )
        copy.start()
        return copy

    def columns(j, k):
        owner = (hi ^ j) * MERGE + (lo ^ k)
        return pl.ds(pl.multiple_of(owner * rows, rows), rows)

    order = list(range(1, outer)) + [0]
    pending = []
    local = []
    got = {}

    def send_columns(j):
        got[j] = [
            remote(a_ref.at[:, columns(j, k)], am.at[j, k], a_sems, (j, k), inner_peer(k))
            for k in range(1, MERGE)
        ]

    send_columns(order[0])
    for j in order:
        local.append(pltpu.make_async_copy(a_ref.at[:, columns(j, 0)], am.at[j, 0], own_sems.at[j]))
    shared = []
    for p, piece in enumerate(moved):
        k = 2 * p
        for j in range(outer):
            local.append(pltpu.make_async_copy(
                piece.at[pl.ds(j * fcols, fcols)], xm.at[j, k], l_sems.at[p, j]))
            shared.append(remote(
                piece.at[pl.ds((outer + j) * fcols, fcols)], xm.at[j, k + 1],
                s_sems, (p, j), inner_peer(1)))
        for i in range(2):
            weights = piece.at[pl.ds(2 * outer * fcols, fcols), pl.ds(i * width, width)]
            local.append(pltpu.make_async_copy(weights, wm.at[i, k], l_sems.at[p, outer + i]))
            shared.append(remote(weights, wm.at[i, k + 1], s_sems, (p, outer + i), inner_peer(1)))
    for copy in local:
        copy.start()
    for copy in local:
        copy.wait()
    for copy in shared:
        copy.wait_recv()
    pending += shared

    merged_cols = MERGE * fcols

    part_rows = rows // PARTS

    def partial_pre(j, c):
        span = slice(c * part_rows, (c + 1) * part_rows)
        total = lax.dot_general(
            xm[j, :, :, span].reshape(merged_cols, part_rows), wm[0].reshape(merged_cols, width),
            (((0,), (0,)), ((), ())), preferred_element_type=jnp.float32)
        if c == 0:
            for copy in got[j]:
                copy.wait_recv()
            pending.extend(got[j])
            if j > 0:
                send_columns(order[order.index(j) + 1])
        return total + lax.dot_general(
            am[j, :, :, span].reshape(merged_cols, part_rows), wm[1].reshape(merged_cols, width),
            (((0,), (0,)), ((), ())), preferred_element_type=jnp.float32)

    def grads(j, c, colsum):
        span = slice(c * part_rows, (c + 1) * part_rows)
        delta = dall[j, span]
        for i, merged in enumerate((xm, am)):
            part = jnp.dot(
                merged[j, :, :, span].reshape(merged_cols, part_rows), delta,
                preferred_element_type=jnp.float32,
            ).reshape(MERGE, fcols, width)
            if j == 0 and c == 0:
                gacc[i] = part
            else:
                gacc[i] = gacc[i] + part
        return colsum + jnp.sum(delta.astype(jnp.float32), axis=0, keepdims=True)

    sent = {}
    for j in range(1, outer):
        for c in range(PARTS):
            span = pl.ds(c * part_rows, part_rows)
            psend[j, span] = partial_pre(j, c).astype(psend.dtype)
            sent[j, c] = remote(
                psend.at[j, span], precv.at[j, span], p_sems, (j, c), outer_peer(j))
    deltas = {}
    for c in range(PARTS):
        span = pl.ds(c * part_rows, part_rows)
        pre = partial_pre(0, c) + bias_ref[...]
        for j in range(1, outer):
            sent[j, c].wait_recv()
            pre = pre + precv[j, span].astype(jnp.float32)
        square = pre * pre
        t = jnp.tanh(ROOT * pre * (1.0 + CUBIC * square))
        half = 0.5 * (1.0 + t)
        slope = half + 0.5 * pre * (1.0 - t * t) * (ROOT * (1.0 + 3.0 * CUBIC * square))
        dall[0, span] = (slope * up_ref[span].astype(jnp.float32)).astype(dall.dtype)
        for j in range(1, outer):
            deltas[j, c] = remote(
                dall.at[0, span], dall.at[j, span], d_sems, (j, c), outer_peer(j))
        hidden_ref[span] = (pre * half).astype(hidden_ref.dtype)
    pending += list(sent.values())
    pending += list(deltas.values())

    colsum = jnp.zeros((1, width), jnp.float32)
    for c in range(PARTS):
        colsum = grads(0, c, colsum)
    for c in range(PARTS):
        for j in range(1, outer):
            deltas[j, c].wait_recv()
            colsum = grads(j, c, colsum)
    row_id = lax.broadcasted_iota(jnp.int32, (16, width), 0)
    tail = slice(2 * fcols, 2 * fcols + 16)

    def split(value):
        high = value.astype(jnp.bfloat16).astype(jnp.float32)
        return jnp.where(
            row_id == 0, high, jnp.where(row_id == 1, value - high, 0.0)).astype(jnp.bfloat16)

    def join(block):
        return jnp.sum(block.astype(jnp.float32), axis=0, keepdims=True)

    tag = split(colsum)
    pairs = MERGE // 2
    sent = {}
    for m in list(range(1, pairs)) + [0]:
        gsend[m, 0:fcols] = gacc[0, 2 * m + 1].astype(gsend.dtype)
        gsend[m, fcols:2 * fcols] = gacc[1, 2 * m + 1].astype(gsend.dtype)
        gsend[m, tail] = tag
        sent[m] = remote(gsend.at[m], gpair.at[m], h_sems, (m,), inner_peer(1))
    passed = {}
    for m in range(1, pairs):
        sent[m].wait_recv()
        if m == 1:
            colsum = colsum + join(gpair[1, tail])
            tag = split(colsum)
        gout[m, 0:fcols] = (gacc[0, 2 * m] + gpair[m, 0:fcols].astype(jnp.float32)).astype(gout.dtype)
        gout[m, fcols:2 * fcols] = (
            gacc[1, 2 * m] + gpair[m, fcols:2 * fcols].astype(jnp.float32)).astype(gout.dtype)
        gout[m, tail] = tag
        passed[m] = remote(gout.at[m], grecv.at[m], g_sems, (m,), inner_peer(2 * m))
    sent[0].wait_recv()
    total_s = gacc[0, 0] + gpair[0, 0:fcols].astype(jnp.float32)
    total_n = gacc[1, 0] + gpair[0, fcols:2 * fcols].astype(jnp.float32)
    for m in range(1, pairs):
        passed[m].wait_recv()
        total_s = total_s + grecv[m, 0:fcols].astype(jnp.float32)
        total_n = total_n + grecv[m, fcols:2 * fcols].astype(jnp.float32)
        colsum = colsum + join(grecv[m, tail])
    pending += list(sent.values())
    pending += list(passed.values())
    vsend[0:fcols] = total_s.astype(vsend.dtype)
    vsend[fcols:2 * fcols] = total_n.astype(vsend.dtype)
    vsend[tail] = split(colsum)
    sent = [remote(vsend, vrecv.at[j], v_sems, (j,), group_peer(j)) for j in range(1, groups)]
    for j in range(1, groups):
        sent[j - 1].wait_recv()
        total_s = total_s + vrecv[j, 0:fcols].astype(jnp.float32)
        total_n = total_n + vrecv[j, fcols:2 * fcols].astype(jnp.float32)
        colsum = colsum + join(vrecv[j, tail])
    pending += sent
    gs_ref[...] = total_s
    gn_ref[...] = total_n
    gb_ref[...] = colsum
    for copy in pending:
        copy.wait_send()


def exchange(moved, aggregated, bias, upstream):
    groups = lax.axis_size("vgroup")
    nfeat = lax.axis_size("feat")
    outer = nfeat // MERGE
    fcols = aggregated.shape[0]
    rows, width = upstream.shape
    any_spec = pl.BlockSpec(memory_space=pl.ANY)
    vmem_spec = pl.BlockSpec(memory_space=pltpu.VMEM)
    dma = pltpu.SemaphoreType.DMA
    return pl.pallas_call(
        functools.partial(exchange_kernel, groups, nfeat),
        out_shape=(
            jax.ShapeDtypeStruct((rows, width), jnp.bfloat16),
            jax.ShapeDtypeStruct((fcols, width), jnp.float32),
            jax.ShapeDtypeStruct((fcols, width), jnp.float32),
            jax.ShapeDtypeStruct((1, width), jnp.float32),
        ),
        in_specs=[any_spec] * (MERGE // 2 + 1) + [vmem_spec] * 2,
        out_specs=(vmem_spec,) * 4,
        scratch_shapes=[
            pltpu.VMEM((outer, MERGE, fcols, rows), jnp.bfloat16),
            pltpu.VMEM((outer, MERGE, fcols, rows), jnp.bfloat16),
            pltpu.VMEM((2, MERGE, fcols, width), jnp.bfloat16),
            pltpu.VMEM((outer, rows, width), jnp.bfloat16),
            pltpu.VMEM((outer, rows, width), jnp.bfloat16),
            pltpu.VMEM((outer, rows, width), jnp.bfloat16),
            pltpu.VMEM((2, MERGE, fcols, width), jnp.float32),
            pltpu.VMEM((MERGE // 2, 2 * fcols + 16, width), jnp.bfloat16),
            pltpu.VMEM((MERGE // 2, 2 * fcols + 16, width), jnp.bfloat16),
            pltpu.VMEM((MERGE // 2, 2 * fcols + 16, width), jnp.bfloat16),
            pltpu.VMEM((MERGE // 2, 2 * fcols + 16, width), jnp.bfloat16),
            pltpu.VMEM((2 * fcols + 16, width), jnp.bfloat16),
            pltpu.VMEM((groups, 2 * fcols + 16, width), jnp.bfloat16),
            dma((2, outer, MERGE)),
            dma((2, MERGE // 2, outer + 2)),
            dma((2, outer, PARTS)),
            dma((2, outer, PARTS)),
            dma((2, MERGE // 2)),
            dma((2, MERGE // 2)),
            dma((2, groups)),
            dma((MERGE // 2, outer + 2)),
            dma((outer,)),
        ],
        compiler_params=pltpu.CompilerParams(
            collective_id=0, has_side_effects=True, vmem_limit_bytes=40 * 2**20),
        name="exchange",
    )(*moved, aggregated, bias.reshape(1, width), upstream)


def body(
    features_t, tile_weights, tile_dst, tile_src, tile_count, w_self, w_neigh, bias, grad_hidden
):
    feats = features_t[0]
    ndst = grad_hidden.shape[0] * lax.axis_size("feat")
    moved = arrange(feats, w_self, w_neigh, grad_hidden.shape[0])
    aggregated = aggregate(feats, tile_weights[0], tile_dst[0], tile_src[0], tile_count, ndst)
    hidden, grad_self, grad_neigh, grad_bias = exchange(moved, aggregated, bias, grad_hidden)
    return (hidden, grad_self, grad_neigh, grad_bias[0])


def solution(mesh):
    return jax.shard_map(
        body,
        mesh=mesh,
        in_specs=(
            P("vgroup", "feat", None),
            P("vgroup", None, None, None),
            P("vgroup", None),
            P("vgroup", None),
            P("vgroup"),
            P("feat", None),
            P("feat", None),
            P(),
            P(("vgroup", "feat"), None),
        ),
        out_specs=(P(("vgroup", "feat"), None), P("feat", None), P("feat", None), P()),
        check_vma=False,
    )
```
